256 devices in a mesh: row: 64 (over x, y_hi, z), col: 4 (over y_lo, core).
Axes of the slice: x: 4, y: 4 (y_hi: 2, y_lo: 2; y = y_hi * 2 + y_lo), z: 8, core: 2. Of those that a mesh axis runs over, the one named last changes fastest.
Arguments:
- east_flow: float32 [768, 128, 768], P('row', 'col'), may hold values from -8 to 8
- north_flow: float32 [768, 128, 768], P('row', 'col'), may hold values from -8 to 8
- upward_flow: float32 [768, 128, 768], P('row', 'col'), may hold values from -8 to 8
- solid: int32 [768, 128, 768], P('row', 'col'), may hold values 0 or 1
- inflow_cells: int32 [4096], replicated, may hold values from 0 to 75497471, as said below
- inflow_speed: float32 [4096], replicated, may hold values from 0.5 to 2
Outputs:
- projected_east: float32 [768, 128, 768], P('row', 'col')
- projected_north: float32 [768, 128, 768], P('row', 'col')
- projected_upward: float32 [768, 128, 768], P('row', 'col')
The draws below stay inside these ranges and needn't reach their ends.
Inputs may be any that keep to these rules, and one draw needn't show every extreme that they name: `inflow_cells`: Distinct; the k-th index lies in [k * 768 * 128 * 768 / 4096, (k + 1) * 768 * 128 * 768 / 4096).
All inputs are finite; a program needn't handle non-finite values. No bound on the sum of `solid` on one device may be relied on, other than what follows from the above.
Results may differ from the reference program's by a relative error of at most 0.0003.
Values sent between devices are 32-bit elements; how exact they have to be, the bound alone decides.
No kernel may reach another device: no remote copies, remote signals or barrier semaphores. Data moves between devices by JAX's collectives and lax.ppermute only.
A program may use at most 128 MiB of HBM per device.

```python
import math
import jax
import jax.numpy as jnp

NX = 768
NY = 768
NZ = 128
INFLOW = 4096


def shaped(values, key):
    return jnp.clip(values, -8.0, 8.0)


def velocity_draw(key, salt):
    key = jax.random.fold_in(key, salt)
    key_values, key_scales = jax.random.split(key)
    values = jax.random.normal(key_values, (NY, NZ, NX), jnp.float32)
    return shaped(values, key_scales)


def draw_east_flow(key, part):
    key = jax.random.fold_in(key, 11)
    return velocity_draw(key, 101)


def draw_north_flow(key, part):
    key = jax.random.fold_in(key, 13)
    return velocity_draw(key, 103)


def draw_upward_flow(key, part):
    key = jax.random.fold_in(key, 17)
    return velocity_draw(key, 107)


def draw_inflow_cells(key, part):
    key = jax.random.fold_in(key, 31)
    stride = NY * NZ * NX // INFLOW
    offsets = jax.random.randint(key, (INFLOW,), 0, stride, dtype=jnp.int32)
    chosen = jnp.arange(INFLOW, dtype=jnp.int32) * stride + offsets
    return chosen.at[0].set(0).at[INFLOW - 1].set(NY * NZ * NX - 1)


def place_ends(drawn, key, low, largest):
    dims = drawn.shape
    place = [jax.random.randint(jax.random.fold_in(key, axis), (), 0, dims[axis]) for axis in range(len(dims))]
    drawn = drawn.at[tuple(place)].set(low)
    longest = dims.index(max(dims))
    place[longest] = (place[longest] + 1) % dims[longest]
    return drawn.at[tuple(place)].set(largest)


def setup_inputs(seed: int = 0) -> dict:
    splits = jax.random.split(jax.random.key(seed), 7)
    east_flow = draw_east_flow(jax.random.fold_in(splits[6], 71), 0)
    north_flow = draw_north_flow(jax.random.fold_in(splits[6], 71), 0)
    upward_flow = draw_upward_flow(jax.random.fold_in(splits[6], 71), 0)
    solid = place_ends((jax.random.randint(splits[3], (NY, NZ, NX), 0, 4) < 1).astype(jnp.int32), jax.random.fold_in(splits[3], 1), 0, 1)
    inflow_cells = draw_inflow_cells(jax.random.fold_in(splits[6], 71), 0)
    inflow_speed = jnp.clip(jax.random.uniform(splits[5], (INFLOW,), jnp.float32, 0.5, 2.0), 0.5, 2.0)
    return {"east_flow": east_flow, "north_flow": north_flow, "upward_flow": upward_flow, "solid": solid, "inflow_cells": inflow_cells, "inflow_speed": inflow_speed}


COEF_ALPHA = 1.0 / 3.0
COEF_A = 14.0 / 9.0
COEF_B = 1.0 / 9.0


def wave_numbers(length):
    indices = jnp.arange(length, dtype=jnp.int32)
    phases = (2.0 * math.pi / length) * indices.astype(jnp.float32)
    modified = (COEF_A * jnp.sin(phases) + 0.5 * COEF_B * jnp.sin(2.0 * phases)) / (1.0 + 2.0 * COEF_ALPHA * jnp.cos(phases))
    nulled = (indices == 0) | (2 * indices == length)
    return jnp.where(nulled, 0.0, modified).astype(jnp.float32), nulled


def derivative(volume, direction):
    length = volume.shape[direction]
    wavenumber, nulled = wave_numbers(length)
    positive = wavenumber[: length // 2 + 1]
    layout = [1, 1, 1]
    layout[direction] = length // 2 + 1
    spectrum = jnp.fft.rfft(volume, axis=direction)
    spectrum = spectrum * (1j * positive.reshape(layout))
    return jnp.fft.irfft(spectrum, n=length, axis=direction).astype(jnp.float32)


def reference(east_flow, north_flow, upward_flow, solid, inflow_cells, inflow_speed):
    fluid = (1 - solid).astype(jnp.float32)
    east_star = east_flow * fluid
    north_star = north_flow * fluid
    upward_star = (upward_flow * fluid).reshape(-1).at[inflow_cells].set(inflow_speed).reshape(upward_flow.shape)
    divergence = derivative(east_star, 2) + derivative(north_star, 0) + derivative(upward_star, 1)
    spectrum = jnp.fft.rfftn(divergence)
    wave_north, null_north = wave_numbers(NY)
    wave_up, null_up = wave_numbers(NZ)
    wave_east, null_east = wave_numbers(NX)
    wave_east = wave_east[: NX // 2 + 1]
    null_east = null_east[: NX // 2 + 1]
    denominator = wave_north[:, None, None] ** 2 + wave_up[None, :, None] ** 2 + wave_east[None, None, :] ** 2
    nulled = null_north[:, None, None] & null_up[None, :, None] & null_east[None, None, :]
    inverse = jnp.where(nulled, 0.0, -1.0 / jnp.where(nulled, 1.0, denominator))
    pressure = jnp.fft.irfftn(spectrum * inverse, s=divergence.shape).astype(jnp.float32)
    projected_east = east_star - derivative(pressure, 2)
    projected_north = north_star - derivative(pressure, 0)
    projected_upward = upward_star - derivative(pressure, 1)
    return projected_east, projected_north, projected_upward
```

```python
import functools

import jax
import jax.numpy as jnp
import numpy as np
from jax import lax
from jax.experimental import pallas as pl
from jax.experimental.pallas import tpu as pltpu
from jax.sharding import PartitionSpec as P

NX, NY, NZ = 768, 768, 128
ROWS, COLS = 64, 4
BY, BZ = NY // ROWS, NZ // COLS
F32, BF16 = jnp.float32, jnp.bfloat16


def wave(n):
    t = 2.0 * np.pi * np.arange(n) / n
    w = (14.0 / 9.0 * np.sin(t) + np.sin(2.0 * t) / 18.0) / (1.0 + 2.0 / 3.0 * np.cos(t))
    w[0] = 0.0
    w[n // 2] = 0.0
    return w


def hartley(n):
    k = np.arange(n)
    a = 2.0 * np.pi / n * (np.outer(k, k) % n)
    return np.cos(a) + np.sin(a)


def split_derivative(n, b):
    k = np.arange(n)
    first = -(np.sin(2.0 * np.pi / n * (np.outer(k, k) % n)) @ wave(n)) / n
    d = -first
    d = -d
    r = (np.sqrt(5.0) - 3.0) / 2.0
    dense = d[(k[:, None] - k[None, :]) % n]
    blocks = n // b
    local = dense[:b, :b]
    c0 = d[2] * (1.0 - r**n) / (r**2 - r ** (n - 2))
    c0 = c0 / (1.0 - r**n)
    extra = d[1] - c0 * (r - r ** (n - 1))
    j = np.arange(b)
    moments = np.zeros((4, b))
    moments[0] = r ** (b - 1 - j)
    moments[1] = r**j
    moments[2, b - 1] = 1.0
    moments[3, 0] = 1.0
    far = np.zeros((n, blocks, 4))
    i = np.arange(b)
    for big_i in range(blocks):
        for big_j in range(blocks):
            if big_i == big_j:
                continue
            gap = (big_i - big_j) % blocks
            rows = slice(big_i * b, (big_i + 1) * b)
            far[rows, big_j, 0] = c0 * r ** (b * gap + i - (b - 1)).astype(np.float64)
            far[rows, big_j, 1] = -c0 * r ** (n - b * gap - i).astype(np.float64)
            if gap == 1:
                far[big_i * b, big_j, 2] = extra
            if gap == blocks - 1:
                far[big_i * b + b - 1, big_j, 3] = -extra
    return dense, local, moments, far


def halves(a):
    a = np.asarray(a, np.float32)
    hi = a.astype(jnp.bfloat16)
    lo = (a - hi.astype(np.float32)).astype(jnp.bfloat16)
    return hi, lo


@functools.lru_cache(maxsize=None)
def constants():
    dense_x = split_derivative(NX, BY)[0]
    _, loc_y, mom_y, far_y = split_derivative(NY, BY)
    _, loc_z, mom_z, far_z = split_derivative(NZ, BZ)
    hx, hy, hz = hartley(NX), hartley(NY), hartley(NZ)
    eye_y, eye_z = np.eye(BY), np.eye(BZ)
    lv_q, lv_m = np.kron(loc_y, eye_z), np.kron(mom_y, eye_z)
    lw_q, lw_m = np.kron(eye_y, loc_z), np.kron(eye_y, mom_z)
    parts = []
    for h in range(2):
        parts.append(np.concatenate([lv_q[h * 192:(h + 1) * 192], lw_q[h * 192:(h + 1) * 192]], 1))
        vm = lv_m[h * 64:(h + 1) * 64]
        parts.append(np.concatenate([vm, np.zeros_like(vm)], 1))
        wm = lw_m[h * 24:(h + 1) * 24]
        parts.append(np.concatenate([np.zeros_like(wm), wm], 1))
    left = np.concatenate(parts, 0)
    far_hz = np.einsum("kz,zcm->kcm", hz, far_z)
    wz = np.zeros((6, NZ, 224))
    for y in range(6):
        wz[y, :, :NZ] = hz
        wide = np.zeros((NZ, COLS, 6, 4))
        wide[:, :, y, :] = far_hz
        wz[y, :, NZ:] = wide.reshape(NZ, 96)
    far_hy = np.einsum("ky,yjm->kjm", hy, far_y)
    wy = np.concatenate([hy.reshape(NY, ROWS, BY), far_hy], 2).reshape(NY, ROWS * 16)
    out = {}
    for name, value in (
        ("hx", hx),
        ("fwd_dx", dense_x.T @ hx),
        ("bwd_dx", hx @ dense_x.T),
        ("left", left),
        ("left_t", left.T),
        ("wz", wz),
        ("wz_t", np.swapaxes(wz, 1, 2)),
        ("wy", wy),
        ("wy_t", wy.T),
    ):
        out[name] = halves(value)
    out["wave2"] = tuple(np.asarray(wave(n) ** 2, np.float32) for n in (NX, NY, NZ))
    return out


def two(a):
    hi = a.astype(BF16)
    return hi, (a - hi.astype(F32)).astype(BF16)


def dot(a, b):
    return jnp.dot(a, b, preferred_element_type=F32)


def dot3(a, b):
    return dot(a[0], b[0]) + (dot(a[0], b[1]) + dot(a[1], b[0]))


def low_half(shape):
    return lax.broadcasted_iota(jnp.int32, shape, len(shape) - 1) < 64


def join(first, second):
    return jnp.where(low_half(first.shape), first, pltpu.roll(second, 64, 1))


def join_high(first, second):
    return jnp.where(low_half(first.shape), pltpu.roll(first, 64, 1), second)


def set_inflow(place, cells, speed, upward):
    def step(t, carry):
        y = t // 2
        row = place[0] * BY + y
        k = (16 * row + 4 * place[1]) // 3 + t % 2
        rel = cells[k] - (row * NZ + place[1] * BZ) * NX
        inside = (rel >= 0) & (rel < BZ * NX)
        rel = jnp.where(inside, rel, 0)
        line = rel // NX
        x = jnp.where(inside, rel - line * NX, -1)
        at = pl.ds(y * BZ + line, 1)
        lanes = lax.broadcasted_iota(jnp.int32, (1, NX), 1)
        upward[at, :] = jnp.where(lanes == x, speed[k], upward[at, :])
        return carry

    lax.fori_loop(0, 2 * BY, step, 0)


def forward_x(place, cells, speed, u, v, w, solid, lh, ll, hh, hl, dh, dl, out, upward, sh, sl):
    fluid = (1 - solid[...]).astype(F32)
    upward[...] = w[...] * fluid
    set_inflow(place, cells, speed, upward)
    u2 = two(u[...] * fluid)
    left = (lh[...], ll[...])
    for n in range(3):
        at = slice(n * 256, (n + 1) * 256)
        both = jnp.concatenate([v[:, at] * fluid[:, at], upward[:, at]], 0)
        s = dot3(left, two(both))
        hi, lo = two(s)
        sh[:, at] = hi
        sl[:, at] = lo
    s2 = (sh[...], sl[...])
    for n in range(3):
        at = slice(n * 256, (n + 1) * 256)
        r = dot3(s2, (hh[:, at], hl[:, at]))
        d = dot3(u2, (dh[:, at], dl[:, at]))
        top = jnp.concatenate([r[:192] + d[:192], r[192:280]], 0)
        bottom = jnp.concatenate([r[280:472] + d[192:], r[472:]], 0)
        for t in range(2):
            a, b = top[:, t * 128:(t + 1) * 128], bottom[:, t * 128:(t + 1) * 128]
            c = 2 * n + t
            if c < 4:
                out[c, :, 0:128] = a
                out[c, :, 128:256] = b
            else:
                c = 2 * (c - 4)
                out[c, :, 256:384] = join(a, b)
                out[c + 1, :, 256:384] = join_high(a, b)


def backward_x(place, cells, speed, u, v, w, solid, x, lh, ll, hh, hl, dh, dl, uo, vo, wo, upward, th, tl, ph, plo):
    fluid = (1 - solid[...]).astype(F32)
    upward[...] = w[...] * fluid
    set_inflow(place, cells, speed, upward)
    for t in range(6):
        if t < 4:
            a, b = x[t, :, 0:128], x[t, :, 128:256]
        else:
            c = 2 * (t - 4)
            e, o = x[c, :, 256:384], x[c + 1, :, 256:384]
            a, b = join(e, o), join_high(e, o)
        hi, lo = two(jnp.concatenate([a, b], 0))
        th[:, t * 128:(t + 1) * 128] = hi
        tl[:, t * 128:(t + 1) * 128] = lo
    t2 = (th[...], tl[...])
    left = (lh[...], ll[...])
    for n in range(3):
        at = slice(n * 256, (n + 1) * 256)
        p = dot3(t2, (hh[:, at], hl[:, at]))
        d = dot3(t2, (dh[:, at], dl[:, at]))
        uo[0:192, at] = u[0:192, at] * fluid[0:192, at] - d[0:192]
        uo[192:384, at] = u[192:384, at] * fluid[192:384, at] - d[280:472]
        g = dot3(left, two(p))
        vo[:, at] = v[:, at] * fluid[:, at] + g[0:384]
        wo[:, at] = upward[:, at] + g[384:768]


def forward_z(x, wh, wl, out):
    marks = [x[c, 256:280, :] for c in range(COLS)]
    for y in range(8):
        own = [x[c, y * 32:(y + 1) * 32, :] for c in range(COLS)]
        if y < 6:
            z = dot3((wh[y], wl[y]), two(jnp.concatenate(own + marks, 0)))
            planes = (y, 6 + y)
        else:
            z = dot3((wh[0, :, 0:128], wl[0, :, 0:128]), two(jnp.concatenate(own, 0)))
            planes = (6 + y, 8 + y)
        a, b = z[0:64], z[64:128]
        for half, plane in enumerate(planes):
            tile = slice(half * 128, (half + 1) * 128)
            pick = join_high if half else join
            third = pick(a[:, 256:384], b[:, 256:384])
            for k, value in enumerate((a[:, tile], b[:, tile], third)):
                out[pl.ds(16 * k + plane, 64, stride=48), :] = value


def backward_z(x, wh, wl, out):
    total = None
    for y in range(8):
        planes = (y, 6 + y) if y < 6 else (6 + y, 8 + y)
        t = [[x[pl.ds(16 * k + p, 64, stride=48), :] for k in range(3)] for p in planes]
        low = jnp.concatenate([t[0][0], t[1][0], join(t[0][2], t[1][2])], 1)
        high = jnp.concatenate([t[0][1], t[1][1], join_high(t[0][2], t[1][2])], 1)
        z = two(jnp.concatenate([low, high], 0))
        if y < 6:
            r = dot3((wh[y], wl[y]), z)
            total = r[128:224] if total is None else total + r[128:224]
        else:
            r = dot3((wh[0, 0:128, :], wl[0, 0:128, :]), z)
        for c in range(COLS):
            out[c, y * 32:(y + 1) * 32, :] = r[c * 32:(c + 1) * 32]
    for c in range(COLS):
        out[c, 256:280, :] = total[c * 24:(c + 1) * 24]


def solve_y(x, kappa2, wave2, ah, al, bh, bl, out):
    tiles = [x[:, 16 * t:16 * (t + 1), :].reshape(ROWS * 16, 128) for t in range(3)]
    s = dot3((ah[...], al[...]), two(jnp.concatenate(tiles, 1)))
    den = wave2[...] + kappa2[...]
    null = den == 0.0
    s = jnp.where(null, 0.0, -s / (jnp.where(null, 1.0, den) * float(NX * NY * NZ)))
    r = dot3((bh[...], bl[...]), two(s))
    for t in range(3):
        out[:, 16 * t:16 * (t + 1), :] = r[:, 128 * t:128 * (t + 1)].reshape(ROWS, 16, 128)


def call(kernel, out_shape, args, scratch=(), scalars=0, flops=10**9):
    spec_v = pl.BlockSpec(memory_space=pltpu.VMEM)
    spec_s = pl.BlockSpec(memory_space=pltpu.SMEM)
    many = isinstance(out_shape, (tuple, list))
    return pl.pallas_call(
        kernel,
        out_shape=out_shape,
        in_specs=[spec_s] * scalars + [spec_v] * (len(args) - scalars),
        out_specs=[spec_v] * len(out_shape) if many else spec_v,
        scratch_shapes=list(scratch),
        compiler_params=pltpu.CompilerParams(vmem_limit_bytes=48 * 2**20),
        name=kernel.__name__,
    )(*args)


def body(east_flow, north_flow, upward_flow, solid, inflow_cells, inflow_speed):
    k = constants()
    row, col = lax.axis_index("row"), lax.axis_index("col")
    place = jnp.stack([row, col]).astype(jnp.int32)
    flat = (BY * BZ, NX)
    fields = [a.reshape(flat) for a in (east_flow, north_flow, upward_flow, solid)]
    sds = jax.ShapeDtypeStruct
    mov = (COLS, 280, 384)
    x = call(
        forward_x, sds(mov, F32),
        [place, inflow_cells, inflow_speed, *fields, *k["left"], *k["hx"], *k["fwd_dx"]],
        [pltpu.VMEM(flat, F32), pltpu.VMEM((560, NX), BF16), pltpu.VMEM((560, NX), BF16)], 3,
    )
    x = lax.all_to_all(x, "col", 0, 0, tiled=True)
    x = call(forward_z, sds((ROWS * 48, 128), F32), [x, *k["wz"]])
    x = lax.all_to_all(x.reshape(ROWS, 48, 128), "row", 0, 0, tiled=True)
    wx2, wy2, wz2 = [jnp.asarray(a) for a in k["wave2"]]
    x128 = lax.dynamic_slice_in_dim(wx2, 128 * col, 128)
    x64 = lax.dynamic_slice_in_dim(wx2, 512 + 64 * col, 64)
    z0 = lax.dynamic_slice_in_dim(wz2, row, 1)
    z1 = lax.dynamic_slice_in_dim(wz2, 64 + row, 1)
    kappa2 = jnp.concatenate([x128 + z0, x128 + z1, x64 + z0, x64 + z1]).reshape(1, 384)
    x = call(solve_y, sds((ROWS, 48, 128), F32), [x, kappa2, wy2.reshape(NY, 1), *k["wy"], *k["wy_t"]])
    x = lax.all_to_all(x, "row", 0, 0, tiled=True).reshape(ROWS * 48, 128)
    x = call(backward_z, sds(mov, F32), [x, *k["wz_t"]])
    x = lax.all_to_all(x, "col", 0, 0, tiled=True)
    outs = call(
        backward_x, [sds(flat, F32)] * 3,
        [place, inflow_cells, inflow_speed, *fields, x, *k["left_t"], *k["hx"], *k["bwd_dx"]],
        [pltpu.VMEM(flat, F32), pltpu.VMEM((560, NX), BF16), pltpu.VMEM((560, NX), BF16),
         pltpu.VMEM((8, 128), F32), pltpu.VMEM((8, 128), F32)], 3,
    )
    return tuple(o.reshape(BY, BZ, NX) for o in outs)


def solution(mesh):
    spec = P("row", "col", None)
    return jax.shard_map(
        body, mesh=mesh, in_specs=(spec,) * 4 + (P(), P()), out_specs=(spec,) * 3, check_vma=False
    )
```

```python
import functools

import jax
import jax.numpy as jnp
import numpy as np
from jax import lax
from jax.experimental import pallas as pl
from jax.experimental.pallas import tpu as pltpu
from jax.sharding import PartitionSpec as P

NX, NY, NZ = 768, 768, 128
ROWS, COLS = 64, 4
BY, BZ = NY // ROWS, NZ // COLS
F32, BF16 = jnp.float32, jnp.bfloat16


def wave(n):
    t = 2.0 * np.pi * np.arange(n) / n
    w = (14.0 / 9.0 * np.sin(t) + np.sin(2.0 * t) / 18.0) / (1.0 + 2.0 / 3.0 * np.cos(t))
    w[0] = 0.0
    w[n // 2] = 0.0
    return w


def hartley(n):
    k = np.arange(n)
    a = 2.0 * np.pi / n * (np.outer(k, k) % n)
    return np.cos(a) + np.sin(a)


def split_derivative(n, b):
    k = np.arange(n)
    first = -(np.sin(2.0 * np.pi / n * (np.outer(k, k) % n)) @ wave(n)) / n
    d = -first
    d = -d
    r = (np.sqrt(5.0) - 3.0) / 2.0
    dense = d[(k[:, None] - k[None, :]) % n]
    blocks = n // b
    local = dense[:b, :b]
    c0 = d[2] * (1.0 - r**n) / (r**2 - r ** (n - 2))
    c0 = c0 / (1.0 - r**n)
    extra = d[1] - c0 * (r - r ** (n - 1))
    j = np.arange(b)
    moments = np.zeros((4, b))
    moments[0] = r ** (b - 1 - j)
    moments[1] = r**j
    moments[2, b - 1] = 1.0
    moments[3, 0] = 1.0
    far = np.zeros((n, blocks, 4))
    i = np.arange(b)
    for big_i in range(blocks):
        for big_j in range(blocks):
            if big_i == big_j:
                continue
            gap = (big_i - big_j) % blocks
            rows = slice(big_i * b, (big_i + 1) * b)
            far[rows, big_j, 0] = c0 * r ** (b * gap + i - (b - 1)).astype(np.float64)
            far[rows, big_j, 1] = -c0 * r ** (n - b * gap - i).astype(np.float64)
            if gap == 1:
                far[big_i * b, big_j, 2] = extra
            if gap == blocks - 1:
                far[big_i * b + b - 1, big_j, 3] = -extra
    return dense, local, moments, far


def halves(a):
    a = np.asarray(a, np.float32)
    hi = a.astype(jnp.bfloat16)
    lo = (a - hi.astype(np.float32)).astype(jnp.bfloat16)
    return hi, lo


RATIO = (np.sqrt(5.0) - 3.0) / 2.0
TAIL, EDGE = 25.0 / 12.0, -1.0 / 12.0


def mode_tables():
    wx, wz = wave(NX), wave(NZ)
    kappa = np.sqrt(wz[:, None] ** 2 + wx[None, :] ** 2).reshape(-1)
    null = kappa == 0.0
    kap = np.where(null, 1.0, kappa)
    c = np.stack([np.full_like(kap, 1 / 36), kap / 3 + 7 / 9, kap, kap / 3 - 7 / 9, np.full_like(kap, -1 / 36)], 1)
    companion = np.zeros((kap.size, 4, 4))
    companion[:, 0, :] = -c[:, 1:] / c[:, :1]
    companion[:, 1, 0] = companion[:, 2, 1] = companion[:, 3, 2] = 1.0
    z = np.sort(np.linalg.eigvals(companion).real, 1)
    c = c[:, :, None]
    for _ in range(3):
        value = (((c[:, 0] * z + c[:, 1]) * z + c[:, 2]) * z + c[:, 3]) * z + c[:, 4]
        slope = ((4 * c[:, 0] * z + 3 * c[:, 1]) * z + 2 * c[:, 2]) * z + c[:, 3]
        z = z - value / slope
    z = np.stack([z[:, 3], 1 / z[:, 1], z[:, 2], 1 / z[:, 0]], 1)
    cos = (z + 1 / z) / 2
    lead = 14 / 9 + cos / 9
    slope = -2 * cos * lead**2 + (1 - cos**2) * 2 * lead / 9 + kap[:, None] ** 2 * 2 * (1 + 2 * cos / 3) * 2 / 3
    a = -((1 + 2 * cos / 3) ** 2) / slope * 2 * z / (1 - z * z)
    a = np.where(null[:, None], 0.0, a) / float(NX * NZ)
    turn = np.where(null[:, None], 1.0, z**BY)
    close = np.where(null[:, None], 1.0, 1 / (1 - z**NY))
    z = np.where(null[:, None], 0.5, z)

    def place(t):
        t = t.reshape(2, ROWS, NX, -1)
        out = np.zeros((COLS, ROWS, 3, 128, t.shape[-1]))
        for c in range(COLS):
            low, high = t[:, :, 128 * c:128 * c + 128], t[:, :, 512 + 64 * c:576 + 64 * c]
            out[c, :, 0], out[c, :, 1] = low[0], low[1]
            out[c, :, 2, :64], out[c, :, 2, 64:] = high[0], high[1]
        return out

    local = place(np.concatenate([z, a], 1)).transpose(0, 4, 2, 1, 3)
    cycle = place(np.concatenate([turn, turn, close, close], 1))
    cycle = cycle.transpose(0, 1, 2, 4, 3).reshape(COLS, ROWS, 3, 2, 8, 128).transpose(0, 1, 3, 2, 4, 5)
    return local.astype(np.float32), np.ascontiguousarray(cycle.reshape(COLS, ROWS, 2, 24, 128)).astype(np.float32)


@functools.lru_cache(maxsize=None)
def null_inverse():
    _, local, moments, _ = split_derivative(NY, BY)
    return np.linalg.pinv(np.concatenate([local, moments], 0))


@functools.lru_cache(maxsize=None)
def constants():
    dense_x = split_derivative(NX, BY)[0]
    _, loc_y, mom_y, far_y = split_derivative(NY, BY)
    _, loc_z, mom_z, far_z = split_derivative(NZ, BZ)
    hx, hy, hz = hartley(NX), hartley(NY), hartley(NZ)
    eye_y, eye_z = np.eye(BY), np.eye(BZ)
    lv_q, lv_m = np.kron(loc_y, eye_z), np.kron(mom_y, eye_z)
    lw_q, lw_m = np.kron(eye_y, loc_z), np.kron(eye_y, mom_z)
    parts = []
    for h in range(2):
        parts.append(np.concatenate([lv_q[h * 192:(h + 1) * 192], lw_q[h * 192:(h + 1) * 192]], 1))
        vm = lv_m[h * 64:(h + 1) * 64]
        parts.append(np.concatenate([vm, np.zeros_like(vm)], 1))
        wm = lw_m[h * 24:(h + 1) * 24]
        parts.append(np.concatenate([np.zeros_like(wm), wm], 1))
    left = np.concatenate(parts, 0)
    far_hz = np.einsum("kz,zcm->kcm", hz, far_z)
    wz = np.zeros((6, NZ, 224))
    for y in range(6):
        wz[y, :, :NZ] = hz
        wide = np.zeros((NZ, COLS, 6, 4))
        wide[:, :, y, :] = far_hz
        wz[y, :, NZ:] = wide.reshape(NZ, 96)
    out = {}
    for name, value in (
        ("hx", hx),
        ("fwd_dx", dense_x.T @ hx),
        ("bwd_dx", hx @ dense_x.T),
        ("left", left),
        ("left_t", left.T),
        ("wz", wz),
        ("wz_t", np.swapaxes(wz, 1, 2)),
    ):
        out[name] = halves(value)
    out["local"], out["cycle"] = mode_tables()
    return out


def two(a):
    hi = a.astype(BF16)
    return hi, (a - hi.astype(F32)).astype(BF16)


def dot(a, b):
    return jnp.dot(a, b, preferred_element_type=F32)


def dot3(a, b):
    return dot(a[0], b[0]) + (dot(a[0], b[1]) + dot(a[1], b[0]))


def low_half(shape):
    return lax.broadcasted_iota(jnp.int32, shape, len(shape) - 1) < 64


def join(first, second):
    return jnp.where(low_half(first.shape), first, pltpu.roll(second, 64, 1))


def join_high(first, second):
    return jnp.where(low_half(first.shape), pltpu.roll(first, 64, 1), second)


def set_inflow(place, cells, speed, upward):
    def step(t, carry):
        y = t // 2
        row = place[0] * BY + y
        k = (16 * row + 4 * place[1]) // 3 + t % 2
        rel = cells[k] - (row * NZ + place[1] * BZ) * NX
        inside = (rel >= 0) & (rel < BZ * NX)
        rel = jnp.where(inside, rel, 0)
        line = rel // NX
        x = jnp.where(inside, rel - line * NX, -1)
        at = pl.ds(y * BZ + line, 1)
        lanes = lax.broadcasted_iota(jnp.int32, (1, NX), 1)
        upward[at, :] = jnp.where(lanes == x, speed[k], upward[at, :])
        return carry

    lax.fori_loop(0, 2 * BY, step, 0)


def forward_x(place, cells, speed, u, v, w, solid, lh, ll, hh, hl, dh, dl, out, upward, sh, sl):
    fluid = (1 - solid[...]).astype(F32)
    upward[...] = w[...] * fluid
    set_inflow(place, cells, speed, upward)
    u2 = two(u[...] * fluid)
    left = (lh[...], ll[...])
    for n in range(3):
        at = slice(n * 256, (n + 1) * 256)
        both = jnp.concatenate([v[:, at] * fluid[:, at], upward[:, at]], 0)
        s = dot3(left, two(both))
        hi, lo = two(s)
        sh[:, at] = hi
        sl[:, at] = lo
    s2 = (sh[...], sl[...])
    for n in range(3):
        at = slice(n * 256, (n + 1) * 256)
        r = dot3(s2, (hh[:, at], hl[:, at]))
        d = dot3(u2, (dh[:, at], dl[:, at]))
        top = jnp.concatenate([r[:192] + d[:192], r[192:280]], 0)
        bottom = jnp.concatenate([r[280:472] + d[192:], r[472:]], 0)
        for t in range(2):
            a, b = top[:, t * 128:(t + 1) * 128], bottom[:, t * 128:(t + 1) * 128]
            c = 2 * n + t
            if c < 4:
                out[c, :, 0:128] = a
                out[c, :, 128:256] = b
            else:
                c = 2 * (c - 4)
                out[c, :, 256:384] = join(a, b)
                out[c + 1, :, 256:384] = join_high(a, b)


def backward_x(place, cells, speed, u, v, w, solid, x, lh, ll, hh, hl, dh, dl, uo, vo, wo, upward, th, tl):
    fluid = (1 - solid[...]).astype(F32)
    upward[...] = w[...] * fluid
    set_inflow(place, cells, speed, upward)
    for t in range(6):
        if t < 4:
            a, b = x[t, :, 0:128], x[t, :, 128:256]
        else:
            c = 2 * (t - 4)
            e, o = x[c, :, 256:384], x[c + 1, :, 256:384]
            a, b = join(e, o), join_high(e, o)
        hi, lo = two(jnp.concatenate([a, b], 0))
        th[:, t * 128:(t + 1) * 128] = hi
        tl[:, t * 128:(t + 1) * 128] = lo
    t2 = (th[...], tl[...])
    left = (lh[...], ll[...])
    for n in range(3):
        at = slice(n * 256, (n + 1) * 256)
        p = dot3(t2, (hh[:, at], hl[:, at]))
        d = dot3(t2, (dh[:, at], dl[:, at]))
        uo[0:192, at] = u[0:192, at] * fluid[0:192, at] - d[0:192]
        uo[192:384, at] = u[192:384, at] * fluid[192:384, at] - d[280:472]
        g = dot3(left, two(p))
        vo[:, at] = v[:, at] * fluid[:, at] + g[0:384]
        wo[:, at] = upward[:, at] + g[384:768]


def forward_z(place, x, wh, wl, table, out, keep, sem):
    copy = pltpu.make_async_copy(table.at[place[1]], keep.at[pl.ds(16, 8)], sem)
    copy.start()
    marks = [x[c, 256:280, :] for c in range(COLS)]
    for y in range(8):
        own = [x[c, y * 32:(y + 1) * 32, :] for c in range(COLS)]
        if y < 6:
            z = dot3((wh[y], wl[y]), two(jnp.concatenate(own + marks, 0)))
            planes = (y, 6 + y)
        else:
            z = dot3((wh[0, :, 0:128], wl[0, :, 0:128]), two(jnp.concatenate(own, 0)))
            planes = (6 + y, 8 + y)
        a, b = z[0:64], z[64:128]
        for half, plane in enumerate(planes):
            tile = slice(half * 128, (half + 1) * 128)
            pick = join_high if half else join
            keep[plane, 0] = a[:, tile]
            keep[plane, 1] = b[:, tile]
            keep[plane, 2] = pick(a[:, 256:384], b[:, 256:384])
    copy.wait()

    def step(j, carry):
        for t in range(3):
            at = lambda p: keep[p, t, pl.ds(8 * j, 8), :]
            q = [at(p) for p in range(BY)]
            plus, minus, last, first = [at(BY + p) for p in range(4)]
            for k in range(4):
                z = at(16 + k)
                near, far = tails(z)
                right = -z * (near * minus + EDGE * first)
                left = z * (near * plus + EDGE * last)
                for i in range(BY):
                    right = z * (right + q[i])
                    left = z * (left + q[BY - 1 - i])
                right = right + (z * far * plus + EDGE * last)
                left = left - (z * far * minus + EDGE * first)
                out[pl.ds(192 * j + 8 * t + k, 8, stride=24), :] = right
                out[pl.ds(192 * j + 8 * t + 4 + k, 8, stride=24), :] = left
        return carry

    lax.fori_loop(0, ROWS // 8, step, 0)
    for t in range(2):
        null = keep[20, t, 0:8, :] == 0.0
        sums = null_sums([keep[p, t, 0:8, :] for p in range(16)])
        for k in range(2):
            for m in (k, 4 + k):
                at = pl.ds(8 * t + m, 8, stride=24)
                out[at, :] = jnp.where(null, sums[k], out[at, :])


def weigh(weights, values):
    return sum(float(w) * value for w, value in zip(weights, values))


def null_sums(planes):
    inverse = null_inverse()
    return weigh(inverse.sum(0), planes), weigh(((-1.0) ** np.arange(BY)) @ inverse, planes)


def null_planes(planes, totals):
    inverse = null_inverse()
    v = [weigh(inverse[i], planes) - (totals[0] + (-1.0) ** i * totals[1]) / float(NY) for i in range(BY)]
    return [weigh(-inverse[:, p] / float(NX * NZ), v) for p in range(16)]


def tails(z):
    return TAIL * RATIO / (1.0 - RATIO * z), TAIL * RATIO / (z - RATIO)


def couple_blocks(place, m, cycle, out, hold):
    ratio = [cycle[0, 0, 0, 8 * t:8 * t + 8, :] for t in range(3)]
    close = [cycle[0, 0, 1, 8 * t:8 * t + 8, :] for t in range(3)]
    upper = lax.broadcasted_iota(jnp.int32, (8, 128), 0) < 4

    def advance(j, s):
        new = []
        for t in range(3):
            rows = slice(8 * t, 8 * t + 8)
            new.append(ratio[t] * s[t] + jnp.where(upper, m[j, rows, :], m[ROWS - 1 - j, rows, :]))
        return tuple(new)

    zero = jnp.zeros((8, 128), F32)
    s = lax.fori_loop(0, ROWS, advance, (zero,) * 3, unroll=4)
    s = tuple(s[t] * close[t] for t in range(3))

    def store(j, s):
        for t in range(3):
            hold[j, 8 * t:8 * t + 8, :] = s[t]
        return advance(j, s)

    lax.fori_loop(0, ROWS, store, s, unroll=4)

    def merge(j, carry):
        for t in range(3):
            rows = slice(8 * t, 8 * t + 8)
            out[j, rows, :] = jnp.where(upper, hold[j, rows, :], hold[ROWS - 1 - j, rows, :])
        return carry

    lax.fori_loop(0, ROWS, merge, 0, unroll=4)


def backward_z(s, keep, wh, wl, out, made):
    def step(j, carry):
        for t in range(3):
            at = lambda p: keep[p, t, pl.ds(8 * j, 8), :]
            state = lambda m: s[pl.ds(192 * j + 8 * t + m, 8, stride=24), :]
            q = [at(p) for p in range(BY)]
            plus, minus, last, first = [at(BY + p) for p in range(4)]
            p = [0.0] * BY
            g = [0.0] * 4
            for k in range(4):
                z, a = at(16 + k), at(20 + k)
                near, far = tails(z)
                from_left, from_right = state(k), state(4 + k)
                right = from_left - z * (near * minus + EDGE * first)
                left = from_right + z * (near * plus + EDGE * last)
                for i in range(BY):
                    right = (right if i == 0 else z * right) + q[i]
                    p[i] = p[i] - a * right
                    back = BY - 1 - i
                    p[back] = p[back] - a * left
                    left = z * (left + q[back])
                right = z * right + (z * far * plus + EDGE * last)
                left = left - (z * far * minus + EDGE * first)
                inverse = 1.0 / z
                g[0] = g[0] - a * (near * right + far * from_right)
                g[1] = g[1] + a * (near * left + far * from_left)
                g[2] = g[2] - a * EDGE * (right + inverse * from_right)
                g[3] = g[3] + a * EDGE * (left + inverse * from_left)
            for i, value in enumerate(p + g):
                made[i, t, pl.ds(8 * j, 8), :] = value
        return carry

    lax.fori_loop(0, ROWS // 8, step, 0)
    for t in range(2):
        null = keep[20, t, 0:8, :] == 0.0
        planes = [keep[p, t, 0:8, :] for p in range(16)]
        own = null_sums(planes)
        state = lambda m: s[pl.ds(8 * t + m, 8, stride=24), :]
        totals = [(own[k] + state(k) + state(4 + k)) / 3.0 for k in range(2)]
        for i, value in enumerate(null_planes(planes, totals)):
            made[i, t, 0:8, :] = jnp.where(null, value, made[i, t, 0:8, :])
    total = None
    for y in range(8):
        planes = (y, 6 + y) if y < 6 else (6 + y, 8 + y)
        t = [[made[p, k] for k in range(3)] for p in planes]
        low = jnp.concatenate([t[0][0], t[1][0], join(t[0][2], t[1][2])], 1)
        high = jnp.concatenate([t[0][1], t[1][1], join_high(t[0][2], t[1][2])], 1)
        z = two(jnp.concatenate([low, high], 0))
        if y < 6:
            r = dot3((wh[y], wl[y]), z)
            total = r[128:224] if total is None else total + r[128:224]
        else:
            r = dot3((wh[0, 0:128, :], wl[0, 0:128, :]), z)
        for c in range(COLS):
            out[c, y * 32:(y + 1) * 32, :] = r[c * 32:(c + 1) * 32]
    for c in range(COLS):
        out[c, 256:280, :] = total[c * 24:(c + 1) * 24]


def call(kernel, out_shape, args, scratch=(), scalars=0, anywhere=()):
    spec_v = pl.BlockSpec(memory_space=pltpu.VMEM)
    spec_s = pl.BlockSpec(memory_space=pltpu.SMEM)
    many = isinstance(out_shape, (tuple, list))
    return pl.pallas_call(
        kernel,
        out_shape=out_shape,
        in_specs=[
            spec_s if i < scalars else pl.BlockSpec(memory_space=pl.ANY) if i in anywhere else spec_v
            for i in range(len(args))
        ],
        out_specs=[spec_v] * len(out_shape) if many else spec_v,
        scratch_shapes=list(scratch),
        compiler_params=pltpu.CompilerParams(vmem_limit_bytes=48 * 2**20),
        name=kernel.__name__,
    )(*args)


def body(east_flow, north_flow, upward_flow, solid, inflow_cells, inflow_speed):
    k = constants()
    row, col = lax.axis_index("row"), lax.axis_index("col")
    place = jnp.stack([row, col]).astype(jnp.int32)
    flat = (BY * BZ, NX)
    fields = [a.reshape(flat) for a in (east_flow, north_flow, upward_flow, solid)]
    sds = jax.ShapeDtypeStruct
    mov = (COLS, 280, 384)
    x = call(
        forward_x, sds(mov, F32),
        [place, inflow_cells, inflow_speed, *fields, *k["left"], *k["hx"], *k["fwd_dx"]],
        [pltpu.VMEM(flat, F32), pltpu.VMEM((560, NX), BF16), pltpu.VMEM((560, NX), BF16)], 3,
    )
    x = lax.all_to_all(x, "col", 0, 0, tiled=True)
    m, keep = call(
        forward_z, (sds((ROWS * 24, 128), F32), sds((24, 3, ROWS, 128), F32)),
        [place, x, *k["wz"], k["local"]], [pltpu.SemaphoreType.DMA], 1, anywhere=(4,),
    )
    m = lax.all_to_all(m.reshape(ROWS, 24, 128), "row", 0, 0, tiled=True)
    m = pl.pallas_call(
        couple_blocks, out_shape=sds((ROWS, 24, 128), F32),
        grid_spec=pltpu.PrefetchScalarGridSpec(
            num_scalar_prefetch=1, grid=(1,),
            in_specs=[pl.BlockSpec((ROWS, 24, 128), lambda i, p: (0, 0, 0)),
                      pl.BlockSpec((1, 1, 2, 24, 128), lambda i, p: (p[1], p[0], 0, 0, 0))],
            out_specs=pl.BlockSpec((ROWS, 24, 128), lambda i, p: (0, 0, 0)),
            scratch_shapes=[pltpu.VMEM((ROWS, 24, 128), F32)],
        ),
        name="couple_blocks",
    )(place, m, k["cycle"])
    m = lax.all_to_all(m, "row", 0, 0, tiled=True).reshape(ROWS * 24, 128)
    x = call(backward_z, sds(mov, F32), [m, keep, *k["wz_t"]], [pltpu.VMEM((16, 3, ROWS, 128), F32)])
    x = lax.all_to_all(x, "col", 0, 0, tiled=True)
    outs = call(
        backward_x, [sds(flat, F32)] * 3,
        [place, inflow_cells, inflow_speed, *fields, x, *k["left_t"], *k["hx"], *k["bwd_dx"]],
        [pltpu.VMEM(flat, F32), pltpu.VMEM((560, NX), BF16), pltpu.VMEM((560, NX), BF16)], 3,
    )
    return tuple(o.reshape(BY, BZ, NX) for o in outs)


def solution(mesh):
    spec = P("row", "col", None)
    return jax.shard_map(
        body, mesh=mesh, in_specs=(spec,) * 4 + (P(), P()), out_specs=(spec,) * 3, check_vma=False
    )
```

```python
import functools

import jax
import jax.numpy as jnp
import numpy as np
from jax import lax
from jax.experimental import pallas as pl
from jax.experimental.pallas import tpu as pltpu
from jax.sharding import PartitionSpec as P

NX, NY, NZ = 768, 768, 128
ROWS, COLS = 64, 4
BY, BZ = NY // ROWS, NZ // COLS
F32, BF16 = jnp.float32, jnp.bfloat16


def wave(n):
    t = 2.0 * np.pi * np.arange(n) / n
    w = (14.0 / 9.0 * np.sin(t) + np.sin(2.0 * t) / 18.0) / (1.0 + 2.0 / 3.0 * np.cos(t))
    w[0] = 0.0
    w[n // 2] = 0.0
    return w


def hartley(n):
    k = np.arange(n)
    a = 2.0 * np.pi / n * (np.outer(k, k) % n)
    return np.cos(a) + np.sin(a)


def split_derivative(n, b):
    k = np.arange(n)
    first = -(np.sin(2.0 * np.pi / n * (np.outer(k, k) % n)) @ wave(n)) / n
    d = -first
    d = -d
    r = (np.sqrt(5.0) - 3.0) / 2.0
    dense = d[(k[:, None] - k[None, :]) % n]
    blocks = n // b
    local = dense[:b, :b]
    c0 = d[2] * (1.0 - r**n) / (r**2 - r ** (n - 2))
    c0 = c0 / (1.0 - r**n)
    extra = d[1] - c0 * (r - r ** (n - 1))
    j = np.arange(b)
    moments = np.zeros((4, b))
    moments[0] = r ** (b - 1 - j)
    moments[1] = r**j
    moments[2, b - 1] = 1.0
    moments[3, 0] = 1.0
    far = np.zeros((n, blocks, 4))
    i = np.arange(b)
    for big_i in range(blocks):
        for big_j in range(blocks):
            if big_i == big_j:
                continue
            gap = (big_i - big_j) % blocks
            rows = slice(big_i * b, (big_i + 1) * b)
            far[rows, big_j, 0] = c0 * r ** (b * gap + i - (b - 1)).astype(np.float64)
            far[rows, big_j, 1] = -c0 * r ** (n - b * gap - i).astype(np.float64)
            if gap == 1:
                far[big_i * b, big_j, 2] = extra
            if gap == blocks - 1:
                far[big_i * b + b - 1, big_j, 3] = -extra
    return dense, local, moments, far


THIRD = NX // 3
ROOT = np.sqrt(3.0)


def thirds_forward(m):
    rows = [m[:THIRD, 0::3]]
    for r in (1, 2):
        top = m[:THIRD, r::3]
        rows += [top, (2.0 * m[THIRD:2 * THIRD, r::3] + top) / ROOT]
    return np.concatenate(rows, 0)


def thirds_backward(m):
    top = np.concatenate([m[1::3, :THIRD], m[2::3, :THIRD]], 0)
    next_third = np.concatenate([m[1::3, THIRD:2 * THIRD], m[2::3, THIRD:2 * THIRD]], 0)
    return np.concatenate([m[0::3, :THIRD], top, (2.0 * next_third + top) / ROOT], 0)


def halves(a):
    a = np.asarray(a, np.float32)
    hi = a.astype(jnp.bfloat16)
    lo = (a - hi.astype(np.float32)).astype(jnp.bfloat16)
    return hi, lo


RATIO = (np.sqrt(5.0) - 3.0) / 2.0
TAIL, EDGE = 25.0 / 12.0, -1.0 / 12.0


def mode_tables():
    wx, wz = wave(NX)[np.arange(NX).reshape(256, 3).T.reshape(-1)], wave(NZ)
    kappa = np.sqrt(wz[:, None] ** 2 + wx[None, :] ** 2).reshape(-1)
    null = kappa == 0.0
    kap = np.where(null, 1.0, kappa)
    c = np.stack([np.full_like(kap, 1 / 36), kap / 3 + 7 / 9, kap, kap / 3 - 7 / 9, np.full_like(kap, -1 / 36)], 1)
    companion = np.zeros((kap.size, 4, 4))
    companion[:, 0, :] = -c[:, 1:] / c[:, :1]
    companion[:, 1, 0] = companion[:, 2, 1] = companion[:, 3, 2] = 1.0
    z = np.sort(np.linalg.eigvals(companion).real, 1)
    c = c[:, :, None]
    for _ in range(3):
        value = (((c[:, 0] * z + c[:, 1]) * z + c[:, 2]) * z + c[:, 3]) * z + c[:, 4]
        slope = ((4 * c[:, 0] * z + 3 * c[:, 1]) * z + 2 * c[:, 2]) * z + c[:, 3]
        z = z - value / slope
    z = np.stack([z[:, 3], 1 / z[:, 1], z[:, 2], 1 / z[:, 0]], 1)
    cos = (z + 1 / z) / 2
    lead = 14 / 9 + cos / 9
    slope = -2 * cos * lead**2 + (1 - cos**2) * 2 * lead / 9 + kap[:, None] ** 2 * 2 * (1 + 2 * cos / 3) * 2 / 3
    a = -((1 + 2 * cos / 3) ** 2) / slope * 2 * z / (1 - z * z)
    a = np.where(null[:, None], 0.0, a) / float(NX * NZ)
    turn = np.where(null[:, None], 1.0, z**BY)
    close = np.where(null[:, None], 1.0, 1 / (1 - z**NY))
    z = np.where(null[:, None], 0.5, z)

    def place(t):
        t = t.reshape(2, ROWS, NX, -1)
        out = np.zeros((COLS, ROWS, 3, 128, t.shape[-1]))
        for c in range(COLS):
            low, high = t[:, :, 128 * c:128 * c + 128], t[:, :, 512 + 64 * c:576 + 64 * c]
            out[c, :, 0], out[c, :, 1] = low[0], low[1]
            out[c, :, 2, :64], out[c, :, 2, 64:] = high[0], high[1]
        return out

    local = place(np.concatenate([z, a], 1)).transpose(0, 4, 2, 1, 3)
    cycle = place(np.concatenate([turn, turn, close, close], 1))
    cycle = cycle.transpose(0, 1, 2, 4, 3).reshape(COLS, ROWS, 3, 2, 8, 128).transpose(0, 1, 3, 2, 4, 5)
    return local.astype(np.float32), np.ascontiguousarray(cycle.reshape(COLS, ROWS, 2, 24, 128)).astype(np.float32)


@functools.lru_cache(maxsize=None)
def null_inverse():
    _, local, moments, _ = split_derivative(NY, BY)
    return np.linalg.pinv(np.concatenate([local, moments], 0))


@functools.lru_cache(maxsize=None)
def constants():
    dense_x = split_derivative(NX, BY)[0]
    _, loc_y, mom_y, far_y = split_derivative(NY, BY)
    _, loc_z, mom_z, far_z = split_derivative(NZ, BZ)
    hx, hy, hz = hartley(NX), hartley(NY), hartley(NZ)
    eye_y, eye_z = np.eye(BY), np.eye(BZ)
    lv_q, lv_m = np.kron(loc_y, eye_z), np.kron(mom_y, eye_z)
    lw_q, lw_m = np.kron(eye_y, loc_z), np.kron(eye_y, mom_z)
    left_v = np.concatenate([lv_m, lv_q, np.zeros_like(lw_m)], 0)
    left_w = np.concatenate([np.zeros_like(lv_m), lw_q, lw_m], 0)
    far_hz = np.einsum("kz,zcm->kcm", hz, far_z)
    wz = np.zeros((6, NZ, 224))
    for y in range(6):
        wz[y, :, :NZ] = hz
        wide = np.zeros((NZ, COLS, 6, 4))
        wide[:, :, y, :] = far_hz
        wz[y, :, NZ:] = wide.reshape(NZ, 96)
    out = {}
    for name, value in (
        ("hx", thirds_forward(hx)),
        ("fwd_dx", thirds_forward(dense_x.T @ hx)),
        ("hx_back", thirds_backward(hx)),
        ("bwd_dx", thirds_backward(hx @ dense_x.T)),
        ("left", np.concatenate([left_v, left_w], 1)),
        ("left_tv", left_v[:512].T),
        ("left_tw", left_w[128:].T),
        ("wz", wz),
        ("wz_t", np.swapaxes(wz, 1, 2)),
    ):
        out[name] = halves(value)
    out["local"], out["cycle"] = mode_tables()
    return out


def two(a):
    hi = a.astype(BF16)
    return hi, (a - hi.astype(F32)).astype(BF16)


def dot(a, b):
    return jnp.dot(a, b, preferred_element_type=F32)


def dot3(a, b):
    return dot(a[0], b[0]) + (dot(a[0], b[1]) + dot(a[1], b[0]))


def low_half(shape):
    return lax.broadcasted_iota(jnp.int32, shape, len(shape) - 1) < 64


def join(first, second):
    return jnp.where(low_half(first.shape), first, pltpu.roll(second, 64, 1))


def join_high(first, second):
    return jnp.where(low_half(first.shape), pltpu.roll(first, 64, 1), second)


def set_inflow(place, cells, speed, upward):
    def step(t, carry):
        y = t // 2
        row = place[0] * BY + y
        k = (16 * row + 4 * place[1]) // 3 + t % 2
        rel = cells[k] - (row * NZ + place[1] * BZ) * NX
        inside = (rel >= 0) & (rel < BZ * NX)
        rel = jnp.where(inside, rel, 0)
        line = rel // NX
        x = jnp.where(inside, rel - line * NX, -1)
        at = pl.ds(y * BZ + line, 1)
        lanes = lax.broadcasted_iota(jnp.int32, (1, NX), 1)
        upward[at, :] = jnp.where(lanes == x, speed[k], upward[at, :])
        return carry

    lax.fori_loop(0, 2 * BY, step, 0)


def fold(parts):
    a, b, c = parts
    return a + (b + c), a - 0.5 * (b + c), (0.5 * ROOT).item() * (b - c)


def unfold(a, b, q):
    low, high = a - 0.5 * b, (0.5 * ROOT).item() * q
    return a + b, low + high, low - high


def forward_x(place, cells, speed, u_in, v_in, w_in, solid_in, lh_in, ll_in, hh_in, hl_in, dh_in, dl_in,
              out, u, v, w, solid, lh, ll, hh, hl, dh, dl, sems):
    pairs = [(solid_in, solid), (w_in, w), (lh_in, lh), (ll_in, ll), (v_in, v),
             (hh_in, hh), (hl_in, hl), (u_in, u), (dh_in, dh), (dl_in, dl)]
    copies = [pltpu.make_async_copy(a, b, sems.at[i]) for i, (a, b) in enumerate(pairs)]
    for copy in copies:
        copy.start()
    for copy in copies[:2]:
        copy.wait()
    fluid = (1 - solid[...]).astype(F32)
    w[...] = w[...] * fluid
    set_inflow(place, cells, speed, w)
    for copy in copies[2:5]:
        copy.wait()
    left = (lh[...], ll[...])
    thirds = []
    for n in range(3):
        at = slice(n * 256, (n + 1) * 256)
        both = jnp.concatenate([v[:, at] * fluid[:, at], w[:, at]], 0)
        thirds.append(dot3(left, two(both)))
    c0, c, d = fold(thirds)
    all_0, all_1 = two(c0), two(jnp.concatenate([c, d], 1))
    for copy in copies[5:8]:
        copy.wait()
    c0, c, d = fold([u[:, n * 256:(n + 1) * 256] * fluid[:, n * 256:(n + 1) * 256] for n in range(3)])
    east_0, east_1 = two(c0), two(jnp.concatenate([c, d], 1))
    for copy in copies[8:]:
        copy.wait()
    for n in range(3):
        at = slice(0, 256) if n == 0 else slice(512 * n - 256, 512 * n + 256)
        r = dot3(all_1 if n else all_0, (hh[at, :], hl[at, :]))
        d = dot3(east_1 if n else east_0, (dh[at, :], dl[at, :]))
        for t in range(2):
            own = slice(t * 128, (t + 1) * 128)
            a = jnp.concatenate([r[128:320, own] + d[:192, own], r[0:64, own], r[512:536, own]], 0)
            b = jnp.concatenate([r[320:512, own] + d[192:, own], r[64:128, own], r[536:560, own]], 0)
            c = 2 * n + t
            if c < 4:
                out[c, :, 0:128] = a
                out[c, :, 128:256] = b
            else:
                c = 2 * (c - 4)
                out[c, :, 256:384] = join(a, b)
                out[c + 1, :, 256:384] = join_high(a, b)


def backward_x(place, cells, speed, u, v, w, solid, x, vh, vl, wh, wl, hh, hl, dh, dl,
               uo, vo, wo, upward, th, tl, us, vs, ws, sems):
    fluid = (1 - solid[...]).astype(F32)
    upward[...] = w[...] * fluid
    set_inflow(place, cells, speed, upward)
    for t in range(6):
        if t < 4:
            a, b = x[t, :, 0:128], x[t, :, 128:256]
        else:
            c = 2 * (t - 4)
            e, o = x[c, :, 256:384], x[c + 1, :, 256:384]
            a, b = join(e, o), join_high(e, o)
        rows = [a[192:256], b[192:256], a[0:192], b[0:192], a[256:280], b[256:280]]
        hi, lo = two(jnp.concatenate(rows, 0))
        th[:, t * 128:(t + 1) * 128] = hi
        tl[:, t * 128:(t + 1) * 128] = lo

    def back(rows, mh, ml):
        first, rest = (th[rows, 0:256], tl[rows, 0:256]), (th[rows, 256:768], tl[rows, 256:768])
        return unfold(*[
            dot3(left, (mh[at, :], ml[at, :]))
            for left, at in ((first, slice(0, 256)), (rest, slice(256, 768)), (rest, slice(768, 1280)))
        ])

    p = back(slice(0, 560), hh, hl)
    d = back(slice(128, 512), dh, dl)
    copies = []

    def send(i, n, stage, target):
        at = pl.ds(n * 256, 256)
        copies.append(pltpu.make_async_copy(stage.at[:, at], target.at[:, at], sems.at[3 * i + n]))
        copies[-1].start()

    for n in range(3):
        at = slice(n * 256, (n + 1) * 256)
        us[:, at] = u[:, at] * fluid[:, at] - d[n]
        send(0, n, us, uo)
    for n in range(3):
        at = slice(n * 256, (n + 1) * 256)
        hi, lo = two(p[n])
        vs[:, at] = v[:, at] * fluid[:, at] + dot3((vh[...], vl[...]), (hi[0:512], lo[0:512]))
        send(1, n, vs, vo)
        ws[:, at] = upward[:, at] + dot3((wh[...], wl[...]), (hi[128:560], lo[128:560]))
        send(2, n, ws, wo)
    for copy in copies:
        copy.wait()


def forward_z(place, x, wh, wl, table, out, keep, sem):
    copy = pltpu.make_async_copy(table.at[place[1]], keep.at[pl.ds(16, 8)], sem)
    copy.start()
    marks = [x[c, 256:280, :] for c in range(COLS)]
    for y in range(8):
        own = [x[c, y * 32:(y + 1) * 32, :] for c in range(COLS)]
        if y < 6:
            z = dot3((wh[y], wl[y]), two(jnp.concatenate(own + marks, 0)))
            planes = (y, 6 + y)
        else:
            z = dot3((wh[0, :, 0:128], wl[0, :, 0:128]), two(jnp.concatenate(own, 0)))
            planes = (6 + y, 8 + y)
        a, b = z[0:64], z[64:128]
        for half, plane in enumerate(planes):
            tile = slice(half * 128, (half + 1) * 128)
            pick = join_high if half else join
            keep[plane, 0] = a[:, tile]
            keep[plane, 1] = b[:, tile]
            keep[plane, 2] = pick(a[:, 256:384], b[:, 256:384])
    copy.wait()

    def step(j, carry):
        for t in range(3):
            at = lambda p: keep[p, t, pl.ds(8 * j, 8), :]
            q = [at(p) for p in range(BY)]
            plus, minus, last, first = [at(BY + p) for p in range(4)]
            for k in range(4):
                z = at(16 + k)
                near, far = tails(z)
                right = -z * (near * minus + EDGE * first)
                left = z * (near * plus + EDGE * last)
                for i in range(BY):
                    right = z * (right + q[i])
                    left = z * (left + q[BY - 1 - i])
                right = right + (z * far * plus + EDGE * last)
                left = left - (z * far * minus + EDGE * first)
                out[pl.ds(192 * j + 8 * t + k, 8, stride=24), :] = right
                out[pl.ds(192 * j + 8 * t + 4 + k, 8, stride=24), :] = left
        return carry

    lax.fori_loop(0, ROWS // 8, step, 0)
    for t in range(2):
        null = keep[20, t, 0:8, :] == 0.0
        sums = null_sums([keep[p, t, 0:8, :] for p in range(16)])
        for k in range(2):
            for m in (k, 4 + k):
                at = pl.ds(8 * t + m, 8, stride=24)
                out[at, :] = jnp.where(null, sums[k], out[at, :])


def weigh(weights, values):
    return sum(float(w) * value for w, value in zip(weights, values))


def null_sums(planes):
    inverse = null_inverse()
    return weigh(inverse.sum(0), planes), weigh(((-1.0) ** np.arange(BY)) @ inverse, planes)


def null_planes(planes, totals):
    inverse = null_inverse()
    v = [weigh(inverse[i], planes) - (totals[0] + (-1.0) ** i * totals[1]) / float(NY) for i in range(BY)]
    return [weigh(-inverse[:, p] / float(NX * NZ), v) for p in range(16)]


def tails(z):
    return TAIL * RATIO / (1.0 - RATIO * z), TAIL * RATIO / (z - RATIO)


def couple_blocks(place, m, cycle, out, hold):
    ratio = [cycle[0, 0, 0, 8 * t:8 * t + 8, :] for t in range(3)]
    close = [cycle[0, 0, 1, 8 * t:8 * t + 8, :] for t in range(3)]
    upper = lax.broadcasted_iota(jnp.int32, (8, 128), 0) < 4

    def advance(j, s):
        new = []
        for t in range(3):
            rows = slice(8 * t, 8 * t + 8)
            new.append(ratio[t] * s[t] + jnp.where(upper, m[j, rows, :], m[ROWS - 1 - j, rows, :]))
        return tuple(new)

    zero = jnp.zeros((8, 128), F32)
    s = lax.fori_loop(0, ROWS, advance, (zero,) * 3, unroll=4)
    s = tuple(s[t] * close[t] for t in range(3))

    def store(j, s):
        for t in range(3):
            hold[j, 8 * t:8 * t + 8, :] = s[t]
        return advance(j, s)

    lax.fori_loop(0, ROWS, store, s, unroll=4)

    def merge(j, carry):
        for t in range(3):
            rows = slice(8 * t, 8 * t + 8)
            out[j, rows, :] = jnp.where(upper, hold[j, rows, :], hold[ROWS - 1 - j, rows, :])
        return carry

    lax.fori_loop(0, ROWS, merge, 0, unroll=4)


def backward_z(s, keep, wh, wl, out, made):
    def step(j, carry):
        for t in range(3):
            at = lambda p: keep[p, t, pl.ds(8 * j, 8), :]
            state = lambda m: s[pl.ds(192 * j + 8 * t + m, 8, stride=24), :]
            q = [at(p) for p in range(BY)]
            plus, minus, last, first = [at(BY + p) for p in range(4)]
            p = [0.0] * BY
            g = [0.0] * 4
            for k in range(4):
                z, a = at(16 + k), at(20 + k)
                near, far = tails(z)
                from_left, from_right = state(k), state(4 + k)
                right = from_left - z * (near * minus + EDGE * first)
                left = from_right + z * (near * plus + EDGE * last)
                for i in range(BY):
                    right = (right if i == 0 else z * right) + q[i]
                    p[i] = p[i] - a * right
                    back = BY - 1 - i
                    p[back] = p[back] - a * left
                    left = z * (left + q[back])
                right = z * right + (z * far * plus + EDGE * last)
                left = left - (z * far * minus + EDGE * first)
                inverse = 1.0 / z
                g[0] = g[0] - a * (near * right + far * from_right)
                g[1] = g[1] + a * (near * left + far * from_left)
                g[2] = g[2] - a * EDGE * (right + inverse * from_right)
                g[3] = g[3] + a * EDGE * (left + inverse * from_left)
            for i, value in enumerate(p + g):
                made[i, t, pl.ds(8 * j, 8), :] = value
        return carry

    lax.fori_loop(0, ROWS // 8, step, 0)
    for t in range(2):
        null = keep[20, t, 0:8, :] == 0.0
        planes = [keep[p, t, 0:8, :] for p in range(16)]
        own = null_sums(planes)
        state = lambda m: s[pl.ds(8 * t + m, 8, stride=24), :]
        totals = [(own[k] + state(k) + state(4 + k)) / 3.0 for k in range(2)]
        for i, value in enumerate(null_planes(planes, totals)):
            made[i, t, 0:8, :] = jnp.where(null, value, made[i, t, 0:8, :])
    total = None
    for y in range(8):
        planes = (y, 6 + y) if y < 6 else (6 + y, 8 + y)
        t = [[made[p, k] for k in range(3)] for p in planes]
        low = jnp.concatenate([t[0][0], t[1][0], join(t[0][2], t[1][2])], 1)
        high = jnp.concatenate([t[0][1], t[1][1], join_high(t[0][2], t[1][2])], 1)
        z = two(jnp.concatenate([low, high], 0))
        if y < 6:
            r = dot3((wh[y], wl[y]), z)
            total = r[128:224] if total is None else total + r[128:224]
        else:
            r = dot3((wh[0, 0:128, :], wl[0, 0:128, :]), z)
        for c in range(COLS):
            out[c, y * 32:(y + 1) * 32, :] = r[c * 32:(c + 1) * 32]
    for c in range(COLS):
        out[c, 256:280, :] = total[c * 24:(c + 1) * 24]


def call(kernel, out_shape, args, scratch=(), scalars=0, anywhere=(), out_space=pltpu.VMEM, vmem=48):
    spec_v = pl.BlockSpec(memory_space=pltpu.VMEM)
    spec_s = pl.BlockSpec(memory_space=pltpu.SMEM)
    many = isinstance(out_shape, (tuple, list))
    return pl.pallas_call(
        kernel,
        out_shape=out_shape,
        in_specs=[
            spec_s if i < scalars else pl.BlockSpec(memory_space=pltpu.HBM) if i in anywhere else spec_v
            for i in range(len(args))
        ],
        out_specs=[pl.BlockSpec(memory_space=out_space)] * len(out_shape) if many else spec_v,
        scratch_shapes=list(scratch),
        compiler_params=pltpu.CompilerParams(vmem_limit_bytes=vmem * 2**20),
        name=kernel.__name__,
    )(*args)


def body(east_flow, north_flow, upward_flow, solid, inflow_cells, inflow_speed):
    k = constants()
    row, col = lax.axis_index("row"), lax.axis_index("col")
    place = jnp.stack([row, col]).astype(jnp.int32)
    flat = (BY * BZ, NX)
    fields = [a.reshape(flat) for a in (east_flow, north_flow, upward_flow, solid)]
    sds = jax.ShapeDtypeStruct
    mov = (COLS, 280, 384)
    x = call(
        forward_x, sds(mov, F32),
        [place, inflow_cells, inflow_speed, *fields, *k["left"], *k["hx"], *k["fwd_dx"]],
        [pltpu.VMEM(flat, F32)] * 3 + [pltpu.VMEM(flat, jnp.int32)] + [pltpu.VMEM((560, NX), BF16)] * 2
        + [pltpu.VMEM((1280, 256), BF16)] * 4 + [pltpu.SemaphoreType.DMA((10,))], 3, range(3, 13), vmem=60,
    )
    x = lax.all_to_all(x, "col", 0, 0, tiled=True)
    m, keep = call(
        forward_z, (sds((ROWS * 24, 128), F32), sds((24, 3, ROWS, 128), F32)),
        [place, x, *k["wz"], k["local"]], [pltpu.SemaphoreType.DMA], 1, anywhere=(4,),
    )
    m = lax.all_to_all(m.reshape(ROWS, 24, 128), "row", 0, 0, tiled=True)
    m = pl.pallas_call(
        couple_blocks, out_shape=sds((ROWS, 24, 128), F32),
        grid_spec=pltpu.PrefetchScalarGridSpec(
            num_scalar_prefetch=1, grid=(1,),
            in_specs=[pl.BlockSpec((ROWS, 24, 128), lambda i, p: (0, 0, 0)),
                      pl.BlockSpec((1, 1, 2, 24, 128), lambda i, p: (p[1], p[0], 0, 0, 0))],
            out_specs=pl.BlockSpec((ROWS, 24, 128), lambda i, p: (0, 0, 0)),
            scratch_shapes=[pltpu.VMEM((ROWS, 24, 128), F32)],
        ),
        name="couple_blocks",
    )(place, m, k["cycle"])
    m = lax.all_to_all(m, "row", 0, 0, tiled=True).reshape(ROWS * 24, 128)
    x = call(backward_z, sds(mov, F32), [m, keep, *k["wz_t"]], [pltpu.VMEM((16, 3, ROWS, 128), F32)])
    x = lax.all_to_all(x, "col", 0, 0, tiled=True)
    outs = call(
        backward_x, [sds(flat, F32)] * 3,
        [place, inflow_cells, inflow_speed, *fields, x, *k["left_tv"], *k["left_tw"], *k["hx_back"], *k["bwd_dx"]],
        [pltpu.VMEM(flat, F32), pltpu.VMEM((560, NX), BF16), pltpu.VMEM((560, NX), BF16)]
        + [pltpu.VMEM(flat, F32)] * 3 + [pltpu.SemaphoreType.DMA((9,))], 3, out_space=pltpu.HBM,
    )
    return tuple(o.reshape(BY, BZ, NX) for o in outs)


def solution(mesh):
    spec = P("row", "col", None)
    return jax.shard_map(
        body, mesh=mesh, in_specs=(spec,) * 4 + (P(), P()), out_specs=(spec,) * 3, check_vma=False
    )
```

```python
import functools

import jax
import jax.numpy as jnp
import numpy as np
from jax import lax
from jax.experimental import pallas as pl
from jax.experimental.pallas import tpu as pltpu
from jax.sharding import PartitionSpec as P

NX, NY, NZ = 768, 768, 128
ROWS, COLS = 64, 4
BY, BZ = NY // ROWS, NZ // COLS
F32, BF16 = jnp.float32, jnp.bfloat16


def wave(n):
    t = 2.0 * np.pi * np.arange(n) / n
    w = (14.0 / 9.0 * np.sin(t) + np.sin(2.0 * t) / 18.0) / (1.0 + 2.0 / 3.0 * np.cos(t))
    w[0] = 0.0
    w[n // 2] = 0.0
    return w


def hartley(n):
    k = np.arange(n)
    a = 2.0 * np.pi / n * (np.outer(k, k) % n)
    return np.cos(a) + np.sin(a)


def split_derivative(n, b):
    k = np.arange(n)
    first = -(np.sin(2.0 * np.pi / n * (np.outer(k, k) % n)) @ wave(n)) / n
    d = -first
    d = -d
    r = (np.sqrt(5.0) - 3.0) / 2.0
    dense = d[(k[:, None] - k[None, :]) % n]
    blocks = n // b
    local = dense[:b, :b]
    c0 = d[2] * (1.0 - r**n) / (r**2 - r ** (n - 2))
    c0 = c0 / (1.0 - r**n)
    extra = d[1] - c0 * (r - r ** (n - 1))
    j = np.arange(b)
    moments = np.zeros((4, b))
    moments[0] = r ** (b - 1 - j)
    moments[1] = r**j
    moments[2, b - 1] = 1.0
    moments[3, 0] = 1.0
    far = np.zeros((n, blocks, 4))
    i = np.arange(b)
    for big_i in range(blocks):
        for big_j in range(blocks):
            if big_i == big_j:
                continue
            gap = (big_i - big_j) % blocks
            rows = slice(big_i * b, (big_i + 1) * b)
            far[rows, big_j, 0] = c0 * r ** (b * gap + i - (b - 1)).astype(np.float64)
            far[rows, big_j, 1] = -c0 * r ** (n - b * gap - i).astype(np.float64)
            if gap == 1:
                far[big_i * b, big_j, 2] = extra
            if gap == blocks - 1:
                far[big_i * b + b - 1, big_j, 3] = -extra
    return dense, local, moments, far


THIRD = NX // 3
ROOT = np.sqrt(3.0)


def thirds_forward(m):
    rows = [m[:THIRD, 0::3]]
    for r in (1, 2):
        top = m[:THIRD, r::3]
        rows += [top, (2.0 * m[THIRD:2 * THIRD, r::3] + top) / ROOT]
    return np.concatenate(rows, 0)


def thirds_backward(m):
    top = np.concatenate([m[1::3, :THIRD], m[2::3, :THIRD]], 0)
    next_third = np.concatenate([m[1::3, THIRD:2 * THIRD], m[2::3, THIRD:2 * THIRD]], 0)
    return np.concatenate([m[0::3, :THIRD], top, (2.0 * next_third + top) / ROOT], 0)


def halves(a):
    a = np.asarray(a, np.float32)
    hi = a.astype(jnp.bfloat16)
    lo = (a - hi.astype(np.float32)).astype(jnp.bfloat16)
    return hi, lo


RATIO = (np.sqrt(5.0) - 3.0) / 2.0
TAIL, EDGE = 25.0 / 12.0, -1.0 / 12.0


def mode_tables():
    wx, wz = wave(NX)[np.arange(NX).reshape(256, 3).T.reshape(-1)], wave(NZ)
    kappa = np.sqrt(wz[:, None] ** 2 + wx[None, :] ** 2).reshape(-1)
    null = kappa == 0.0
    kap = np.where(null, 1.0, kappa)
    c = np.stack([np.full_like(kap, 1 / 36), kap / 3 + 7 / 9, kap, kap / 3 - 7 / 9, np.full_like(kap, -1 / 36)], 1)
    companion = np.zeros((kap.size, 4, 4))
    companion[:, 0, :] = -c[:, 1:] / c[:, :1]
    companion[:, 1, 0] = companion[:, 2, 1] = companion[:, 3, 2] = 1.0
    z = np.sort(np.linalg.eigvals(companion).real, 1)
    c = c[:, :, None]
    for _ in range(3):
        value = (((c[:, 0] * z + c[:, 1]) * z + c[:, 2]) * z + c[:, 3]) * z + c[:, 4]
        slope = ((4 * c[:, 0] * z + 3 * c[:, 1]) * z + 2 * c[:, 2]) * z + c[:, 3]
        z = z - value / slope
    z = np.stack([z[:, 3], 1 / z[:, 1], z[:, 2], 1 / z[:, 0]], 1)
    cos = (z + 1 / z) / 2
    lead = 14 / 9 + cos / 9
    slope = -2 * cos * lead**2 + (1 - cos**2) * 2 * lead / 9 + kap[:, None] ** 2 * 2 * (1 + 2 * cos / 3) * 2 / 3
    a = -((1 + 2 * cos / 3) ** 2) / slope * 2 * z / (1 - z * z)
    a = np.where(null[:, None], 0.0, a) / float(NX * NZ)
    turn = np.where(null[:, None], 1.0, z**BY)
    close = np.where(null[:, None], 1.0, 1 / (1 - z**NY))
    z = np.where(null[:, None], 0.5, z)

    def place(t):
        t = t.reshape(2, ROWS, NX, -1)
        out = np.zeros((COLS, ROWS, 3, 128, t.shape[-1]))
        for c in range(COLS):
            low, high = t[:, :, 128 * c:128 * c + 128], t[:, :, 512 + 64 * c:576 + 64 * c]
            out[c, :, 0], out[c, :, 1] = low[0], low[1]
            out[c, :, 2, :64], out[c, :, 2, 64:] = high[0], high[1]
        return out

    local = place(np.concatenate([z, a], 1)).transpose(0, 4, 2, 1, 3)
    cycle = place(np.concatenate([turn, turn, close, close], 1))
    cycle = cycle.transpose(0, 1, 2, 4, 3).reshape(COLS, ROWS, 3, 2, 8, 128).transpose(0, 1, 3, 2, 4, 5)
    return local.astype(np.float32), np.ascontiguousarray(cycle.reshape(COLS, ROWS, 2, 24, 128)).astype(np.float32)


@functools.lru_cache(maxsize=None)
def null_inverse():
    _, local, moments, _ = split_derivative(NY, BY)
    return np.linalg.pinv(np.concatenate([local, moments], 0))


@functools.lru_cache(maxsize=None)
def constants():
    dense_x = split_derivative(NX, BY)[0]
    _, loc_y, mom_y, far_y = split_derivative(NY, BY)
    _, loc_z, mom_z, far_z = split_derivative(NZ, BZ)
    hx, hy, hz = hartley(NX), hartley(NY), hartley(NZ)
    eye_y, eye_z = np.eye(BY), np.eye(BZ)
    lv_q, lv_m = np.kron(loc_y, eye_z), np.kron(mom_y, eye_z)
    lw_q, lw_m = np.kron(eye_y, loc_z), np.kron(eye_y, mom_z)
    left_v = np.concatenate([lv_m, lv_q, np.zeros_like(lw_m)], 0)
    left_w = np.concatenate([np.zeros_like(lv_m), lw_q, lw_m], 0)
    far_hz = np.einsum("kz,zcm->kcm", hz, far_z)
    wz = np.zeros((6, NZ, 224))
    for y in range(6):
        wz[y, :, :NZ] = hz
        wide = np.zeros((NZ, COLS, 6, 4))
        wide[:, :, y, :] = far_hz
        wz[y, :, NZ:] = wide.reshape(NZ, 96)
    out = {}
    for name, value in (
        ("hx", thirds_forward(hx)),
        ("fwd_dx", thirds_forward(dense_x.T @ hx)),
        ("hx_back", thirds_backward(hx)),
        ("bwd_dx", thirds_backward(hx @ dense_x.T)),
        ("left", np.concatenate([left_v, left_w], 1)),
        ("left_tv", left_v[:512].T),
        ("left_tw", left_w[128:].T),
        ("wz", wz),
        ("wz_t", np.swapaxes(wz, 1, 2)),
    ):
        out[name] = halves(value)
    out["local"], out["cycle"] = mode_tables()
    return out


def two(a):
    hi = a.astype(BF16)
    return hi, (a - hi.astype(F32)).astype(BF16)


def dot(a, b):
    return jnp.dot(a, b, preferred_element_type=F32)


def dot3(a, b):
    return dot(a[0], b[0]) + (dot(a[0], b[1]) + dot(a[1], b[0]))


def low_half(shape):
    return lax.broadcasted_iota(jnp.int32, shape, len(shape) - 1) < 64


def join(first, second):
    return jnp.where(low_half(first.shape), first, pltpu.roll(second, 64, 1))


def join_high(first, second):
    return jnp.where(low_half(first.shape), pltpu.roll(first, 64, 1), second)


def set_inflow(place, cells, speed, upward):
    def step(t, carry):
        y = t // 2
        row = place[0] * BY + y
        k = (16 * row + 4 * place[1]) // 3 + t % 2
        rel = cells[k] - (row * NZ + place[1] * BZ) * NX
        inside = (rel >= 0) & (rel < BZ * NX)
        rel = jnp.where(inside, rel, 0)
        line = rel // NX
        x = jnp.where(inside, rel - line * NX, -1)
        at = pl.ds(y * BZ + line, 1)
        lanes = lax.broadcasted_iota(jnp.int32, (1, NX), 1)
        upward[at, :] = jnp.where(lanes == x, speed[k], upward[at, :])
        return carry

    lax.fori_loop(0, 2 * BY, step, 0)


def fold(parts):
    a, b, c = parts
    return a + (b + c), a - 0.5 * (b + c), (0.5 * ROOT).item() * (b - c)


def unfold(a, b, q):
    low, high = a - 0.5 * b, (0.5 * ROOT).item() * q
    return a + b, low + high, low - high


def deal(place, blocks, outs):
    for d, out in enumerate(outs):
        out[...] = blocks[place[1] ^ d]


def collect(place, ins, blocks):
    for d, block in enumerate(ins):
        blocks[place[1] ^ d] = block[...]


def exchange(blocks):
    moved = {d: lax.ppermute(blocks[d], "col", [(c, c ^ d) for c in range(COLS)]) for d in (2, 3, 1)}
    return [blocks[0], moved[1], moved[2], moved[3]]


def forward_x(place, cells, speed, u_in, v_in, w_in, solid_in, lh_in, ll_in, hh_in, hl_in, dh_in, dl_in,
              o0, o1, o2, o3, out, u, v, w, solid, lh, ll, hh, hl, dh, dl, sems):
    pairs = [(solid_in, solid), (w_in, w), (lh_in, lh), (ll_in, ll), (v_in, v),
             (hh_in, hh), (hl_in, hl), (u_in, u), (dh_in, dh), (dl_in, dl)]
    copies = [pltpu.make_async_copy(a, b, sems.at[i]) for i, (a, b) in enumerate(pairs)]
    for copy in copies:
        copy.start()
    for copy in copies[:2]:
        copy.wait()
    fluid = (1 - solid[...]).astype(F32)
    w[...] = w[...] * fluid
    set_inflow(place, cells, speed, w)
    for copy in copies[2:5]:
        copy.wait()
    left = (lh[...], ll[...])
    thirds = []
    for n in range(3):
        at = slice(n * 256, (n + 1) * 256)
        both = jnp.concatenate([v[:, at] * fluid[:, at], w[:, at]], 0)
        thirds.append(dot3(left, two(both)))
    c0, c, d = fold(thirds)
    all_0, all_1 = two(c0), two(jnp.concatenate([c, d], 1))
    for copy in copies[5:8]:
        copy.wait()
    c0, c, d = fold([u[:, n * 256:(n + 1) * 256] * fluid[:, n * 256:(n + 1) * 256] for n in range(3)])
    east_0, east_1 = two(c0), two(jnp.concatenate([c, d], 1))
    for copy in copies[8:]:
        copy.wait()
    for n in range(3):
        at = slice(0, 256) if n == 0 else slice(512 * n - 256, 512 * n + 256)
        r = dot3(all_1 if n else all_0, (hh[at, :], hl[at, :]))
        d = dot3(east_1 if n else east_0, (dh[at, :], dl[at, :]))
        for t in range(2):
            own = slice(t * 128, (t + 1) * 128)
            a = jnp.concatenate([r[128:320, own] + d[:192, own], r[0:64, own], r[512:536, own]], 0)
            b = jnp.concatenate([r[320:512, own] + d[192:, own], r[64:128, own], r[536:560, own]], 0)
            c = 2 * n + t
            if c < 4:
                out[c, :, 0:128] = a
                out[c, :, 128:256] = b
            else:
                c = 2 * (c - 4)
                out[c, :, 256:384] = join(a, b)
                out[c + 1, :, 256:384] = join_high(a, b)
    deal(place, out, (o0, o1, o2, o3))


def backward_x(place, cells, speed, u, v, w, solid, x0, x1, x2, x3, vh, vl, wh, wl, hh, hl, dh, dl,
               uo, vo, wo, x, upward, th, tl, us, vs, ws, sems):
    fluid = (1 - solid[...]).astype(F32)
    upward[...] = w[...] * fluid
    set_inflow(place, cells, speed, upward)
    collect(place, (x0, x1, x2, x3), x)
    for t in range(6):
        if t < 4:
            a, b = x[t, :, 0:128], x[t, :, 128:256]
        else:
            c = 2 * (t - 4)
            e, o = x[c, :, 256:384], x[c + 1, :, 256:384]
            a, b = join(e, o), join_high(e, o)
        rows = [a[192:256], b[192:256], a[0:192], b[0:192], a[256:280], b[256:280]]
        hi, lo = two(jnp.concatenate(rows, 0))
        th[:, t * 128:(t + 1) * 128] = hi
        tl[:, t * 128:(t + 1) * 128] = lo

    def back(rows, mh, ml):
        first, rest = (th[rows, 0:256], tl[rows, 0:256]), (th[rows, 256:768], tl[rows, 256:768])
        return unfold(*[
            dot3(left, (mh[at, :], ml[at, :]))
            for left, at in ((first, slice(0, 256)), (rest, slice(256, 768)), (rest, slice(768, 1280)))
        ])

    p = back(slice(0, 560), hh, hl)
    d = back(slice(128, 512), dh, dl)
    copies = []

    def send(i, n, stage, target):
        at = pl.ds(n * 256, 256)
        copies.append(pltpu.make_async_copy(stage.at[:, at], target.at[:, at], sems.at[3 * i + n]))
        copies[-1].start()

    for n in range(3):
        at = slice(n * 256, (n + 1) * 256)
        us[:, at] = u[:, at] * fluid[:, at] - d[n]
        send(0, n, us, uo)
    for n in range(3):
        at = slice(n * 256, (n + 1) * 256)
        hi, lo = two(p[n])
        vs[:, at] = v[:, at] * fluid[:, at] + dot3((vh[...], vl[...]), (hi[0:512], lo[0:512]))
        send(1, n, vs, vo)
        ws[:, at] = upward[:, at] + dot3((wh[...], wl[...]), (hi[128:560], lo[128:560]))
        send(2, n, ws, wo)
    for copy in copies:
        copy.wait()


def forward_z(place, x0, x1, x2, x3, wh, wl, table, out, keep, x, sem):
    copy = pltpu.make_async_copy(table.at[place[1]], keep.at[pl.ds(16, 8)], sem)
    copy.start()
    collect(place, (x0, x1, x2, x3), x)
    marks = [x[c, 256:280, :] for c in range(COLS)]
    for y in range(8):
        own = [x[c, y * 32:(y + 1) * 32, :] for c in range(COLS)]
        if y < 6:
            z = dot3((wh[y], wl[y]), two(jnp.concatenate(own + marks, 0)))
            planes = (y, 6 + y)
        else:
            z = dot3((wh[0, :, 0:128], wl[0, :, 0:128]), two(jnp.concatenate(own, 0)))
            planes = (6 + y, 8 + y)
        a, b = z[0:64], z[64:128]
        for half, plane in enumerate(planes):
            tile = slice(half * 128, (half + 1) * 128)
            pick = join_high if half else join
            keep[plane, 0] = a[:, tile]
            keep[plane, 1] = b[:, tile]
            keep[plane, 2] = pick(a[:, 256:384], b[:, 256:384])
    copy.wait()

    def step(j, carry):
        for t in range(3):
            at = lambda p: keep[p, t, pl.ds(8 * j, 8), :]
            q = [at(p) for p in range(BY)]
            plus, minus, last, first = [at(BY + p) for p in range(4)]
            for k in range(4):
                z = at(16 + k)
                near, far = tails(z)
                right = -z * (near * minus + EDGE * first)
                left = z * (near * plus + EDGE * last)
                for i in range(BY):
                    right = z * (right + q[i])
                    left = z * (left + q[BY - 1 - i])
                right = right + (z * far * plus + EDGE * last)
                left = left - (z * far * minus + EDGE * first)
                out[pl.ds(192 * j + 8 * t + k, 8, stride=24), :] = right
                out[pl.ds(192 * j + 8 * t + 4 + k, 8, stride=24), :] = left
        return carry

    lax.fori_loop(0, ROWS // 8, step, 0)
    for t in range(2):
        null = keep[20, t, 0:8, :] == 0.0
        sums = null_sums([keep[p, t, 0:8, :] for p in range(16)])
        for k in range(2):
            for m in (k, 4 + k):
                at = pl.ds(8 * t + m, 8, stride=24)
                out[at, :] = jnp.where(null, sums[k], out[at, :])


def weigh(weights, values):
    return sum(float(w) * value for w, value in zip(weights, values))


def null_sums(planes):
    inverse = null_inverse()
    return weigh(inverse.sum(0), planes), weigh(((-1.0) ** np.arange(BY)) @ inverse, planes)


def null_planes(planes, totals):
    inverse = null_inverse()
    v = [weigh(inverse[i], planes) - (totals[0] + (-1.0) ** i * totals[1]) / float(NY) for i in range(BY)]
    return [weigh(-inverse[:, p] / float(NX * NZ), v) for p in range(16)]


def tails(z):
    return TAIL * RATIO / (1.0 - RATIO * z), TAIL * RATIO / (z - RATIO)


def couple_blocks(place, m, cycle, out, hold):
    ratio = [cycle[0, 0, 0, 8 * t:8 * t + 8, :] for t in range(3)]
    close = [cycle[0, 0, 1, 8 * t:8 * t + 8, :] for t in range(3)]
    upper = lax.broadcasted_iota(jnp.int32, (8, 128), 0) < 4

    def advance(j, s):
        new = []
        for t in range(3):
            rows = slice(8 * t, 8 * t + 8)
            new.append(ratio[t] * s[t] + jnp.where(upper, m[j, rows, :], m[ROWS - 1 - j, rows, :]))
        return tuple(new)

    zero = jnp.zeros((8, 128), F32)
    s = lax.fori_loop(0, ROWS, advance, (zero,) * 3, unroll=4)
    s = tuple(s[t] * close[t] for t in range(3))

    def store(j, s):
        for t in range(3):
            hold[j, 8 * t:8 * t + 8, :] = s[t]
        return advance(j, s)

    lax.fori_loop(0, ROWS, store, s, unroll=4)

    def merge(j, carry):
        for t in range(3):
            rows = slice(8 * t, 8 * t + 8)
            out[j, rows, :] = jnp.where(upper, hold[j, rows, :], hold[ROWS - 1 - j, rows, :])
        return carry

    lax.fori_loop(0, ROWS, merge, 0, unroll=4)


def backward_z(place, s, keep, wh, wl, o0, o1, o2, o3, out, made):
    def step(j, carry):
        for t in range(3):
            at = lambda p: keep[p, t, pl.ds(8 * j, 8), :]
            state = lambda m: s[pl.ds(192 * j + 8 * t + m, 8, stride=24), :]
            q = [at(p) for p in range(BY)]
            plus, minus, last, first = [at(BY + p) for p in range(4)]
            p = [0.0] * BY
            g = [0.0] * 4
            for k in range(4):
                z, a = at(16 + k), at(20 + k)
                near, far = tails(z)
                from_left, from_right = state(k), state(4 + k)
                right = from_left - z * (near * minus + EDGE * first)
                left = from_right + z * (near * plus + EDGE * last)
                for i in range(BY):
                    right = (right if i == 0 else z * right) + q[i]
                    p[i] = p[i] - a * right
                    back = BY - 1 - i
                    p[back] = p[back] - a * left
                    left = z * (left + q[back])
                right = z * right + (z * far * plus + EDGE * last)
                left = left - (z * far * minus + EDGE * first)
                inverse = 1.0 / z
                g[0] = g[0] - a * (near * right + far * from_right)
                g[1] = g[1] + a * (near * left + far * from_left)
                g[2] = g[2] - a * EDGE * (right + inverse * from_right)
                g[3] = g[3] + a * EDGE * (left + inverse * from_left)
            for i, value in enumerate(p + g):
                made[i, t, pl.ds(8 * j, 8), :] = value
        return carry

    lax.fori_loop(0, ROWS // 8, step, 0)
    for t in range(2):
        null = keep[20, t, 0:8, :] == 0.0
        planes = [keep[p, t, 0:8, :] for p in range(16)]
        own = null_sums(planes)
        state = lambda m: s[pl.ds(8 * t + m, 8, stride=24), :]
        totals = [(own[k] + state(k) + state(4 + k)) / 3.0 for k in range(2)]
        for i, value in enumerate(null_planes(planes, totals)):
            made[i, t, 0:8, :] = jnp.where(null, value, made[i, t, 0:8, :])
    total = None
    for y in range(8):
        planes = (y, 6 + y) if y < 6 else (6 + y, 8 + y)
        t = [[made[p, k] for k in range(3)] for p in planes]
        low = jnp.concatenate([t[0][0], t[1][0], join(t[0][2], t[1][2])], 1)
        high = jnp.concatenate([t[0][1], t[1][1], join_high(t[0][2], t[1][2])], 1)
        z = two(jnp.concatenate([low, high], 0))
        if y < 6:
            r = dot3((wh[y], wl[y]), z)
            total = r[128:224] if total is None else total + r[128:224]
        else:
            r = dot3((wh[0, 0:128, :], wl[0, 0:128, :]), z)
        for c in range(COLS):
            out[c, y * 32:(y + 1) * 32, :] = r[c * 32:(c + 1) * 32]
    for c in range(COLS):
        out[c, 256:280, :] = total[c * 24:(c + 1) * 24]
    deal(place, out, (o0, o1, o2, o3))


def call(kernel, out_shape, args, scratch=(), scalars=0, anywhere=(), out_space=pltpu.VMEM, vmem=48):
    spec_v = pl.BlockSpec(memory_space=pltpu.VMEM)
    spec_s = pl.BlockSpec(memory_space=pltpu.SMEM)
    many = isinstance(out_shape, (tuple, list))
    return pl.pallas_call(
        kernel,
        out_shape=out_shape,
        in_specs=[
            spec_s if i < scalars else pl.BlockSpec(memory_space=pltpu.HBM) if i in anywhere else spec_v
            for i in range(len(args))
        ],
        out_specs=[pl.BlockSpec(memory_space=out_space)] * len(out_shape) if many else spec_v,
        scratch_shapes=list(scratch),
        compiler_params=pltpu.CompilerParams(vmem_limit_bytes=vmem * 2**20),
        name=kernel.__name__,
    )(*args)


def body(east_flow, north_flow, upward_flow, solid, inflow_cells, inflow_speed):
    k = constants()
    row, col = lax.axis_index("row"), lax.axis_index("col")
    place = jnp.stack([row, col]).astype(jnp.int32)
    flat = (BY * BZ, NX)
    fields = [a.reshape(flat) for a in (east_flow, north_flow, upward_flow, solid)]
    sds = jax.ShapeDtypeStruct
    mov = (COLS, 280, 384)
    x = call(
        forward_x, [sds(mov[1:], F32)] * COLS,
        [place, inflow_cells, inflow_speed, *fields, *k["left"], *k["hx"], *k["fwd_dx"]],
        [pltpu.VMEM(mov, F32)] + [pltpu.VMEM(flat, F32)] * 3 + [pltpu.VMEM(flat, jnp.int32)] + [pltpu.VMEM((560, NX), BF16)] * 2
        + [pltpu.VMEM((1280, 256), BF16)] * 4 + [pltpu.SemaphoreType.DMA((10,))], 3, range(3, 13), vmem=60,
    )
    x = exchange(x)
    m, keep = call(
        forward_z, (sds((ROWS * 24, 128), F32), sds((24, 3, ROWS, 128), F32)),
        [place, *x, *k["wz"], k["local"]], [pltpu.VMEM(mov, F32), pltpu.SemaphoreType.DMA], 1, anywhere=(7,),
    )
    m = lax.all_to_all(m.reshape(ROWS, 24, 128), "row", 0, 0, tiled=True)
    m = pl.pallas_call(
        couple_blocks, out_shape=sds((ROWS, 24, 128), F32),
        grid_spec=pltpu.PrefetchScalarGridSpec(
            num_scalar_prefetch=1, grid=(1,),
            in_specs=[pl.BlockSpec((ROWS, 24, 128), lambda i, p: (0, 0, 0)),
                      pl.BlockSpec((1, 1, 2, 24, 128), lambda i, p: (p[1], p[0], 0, 0, 0))],
            out_specs=pl.BlockSpec((ROWS, 24, 128), lambda i, p: (0, 0, 0)),
            scratch_shapes=[pltpu.VMEM((ROWS, 24, 128), F32)],
        ),
        name="couple_blocks",
    )(place, m, k["cycle"])
    m = lax.all_to_all(m, "row", 0, 0, tiled=True).reshape(ROWS * 24, 128)
    x = call(
        backward_z, [sds(mov[1:], F32)] * COLS, [place, m, keep, *k["wz_t"]],
        [pltpu.VMEM(mov, F32), pltpu.VMEM((16, 3, ROWS, 128), F32)], 1,
    )
    x = exchange(x)
    outs = call(
        backward_x, [sds(flat, F32)] * 3,
        [place, inflow_cells, inflow_speed, *fields, *x, *k["left_tv"], *k["left_tw"], *k["hx_back"], *k["bwd_dx"]],
        [pltpu.VMEM(mov, F32), pltpu.VMEM(flat, F32), pltpu.VMEM((560, NX), BF16), pltpu.VMEM((560, NX), BF16)]
        + [pltpu.VMEM(flat, F32)] * 3 + [pltpu.SemaphoreType.DMA((9,))], 3, out_space=pltpu.HBM,
    )
    return tuple(o.reshape(BY, BZ, NX) for o in outs)


def solution(mesh):
    spec = P("row", "col", None)
    return jax.shard_map(
        body, mesh=mesh, in_specs=(spec,) * 4 + (P(), P()), out_specs=(spec,) * 3, check_vma=False
    )
```

```python
import functools

import jax
import jax.numpy as jnp
import numpy as np
from jax import lax
from jax.experimental import pallas as pl
from jax.experimental.pallas import tpu as pltpu
from jax.sharding import PartitionSpec as P

NX, NY, NZ = 768, 768, 128
ROWS, COLS = 64, 4
BY, BZ = NY // ROWS, NZ // COLS
F32, BF16 = jnp.float32, jnp.bfloat16


def wave(n):
    t = 2.0 * np.pi * np.arange(n) / n
    w = (14.0 / 9.0 * np.sin(t) + np.sin(2.0 * t) / 18.0) / (1.0 + 2.0 / 3.0 * np.cos(t))
    w[0] = 0.0
    w[n // 2] = 0.0
    return w


def hartley(n):
    k = np.arange(n)
    a = 2.0 * np.pi / n * (np.outer(k, k) % n)
    return np.cos(a) + np.sin(a)


def split_derivative(n, b):
    k = np.arange(n)
    first = -(np.sin(2.0 * np.pi / n * (np.outer(k, k) % n)) @ wave(n)) / n
    d = -first
    d = -d
    r = (np.sqrt(5.0) - 3.0) / 2.0
    dense = d[(k[:, None] - k[None, :]) % n]
    blocks = n // b
    local = dense[:b, :b]
    c0 = d[2] * (1.0 - r**n) / (r**2 - r ** (n - 2))
    c0 = c0 / (1.0 - r**n)
    extra = d[1] - c0 * (r - r ** (n - 1))
    j = np.arange(b)
    moments = np.zeros((4, b))
    moments[0] = r ** (b - 1 - j)
    moments[1] = r**j
    moments[2, b - 1] = 1.0
    moments[3, 0] = 1.0
    far = np.zeros((n, blocks, 4))
    i = np.arange(b)
    for big_i in range(blocks):
        for big_j in range(blocks):
            if big_i == big_j:
                continue
            gap = (big_i - big_j) % blocks
            rows = slice(big_i * b, (big_i + 1) * b)
            far[rows, big_j, 0] = c0 * r ** (b * gap + i - (b - 1)).astype(np.float64)
            far[rows, big_j, 1] = -c0 * r ** (n - b * gap - i).astype(np.float64)
            if gap == 1:
                far[big_i * b, big_j, 2] = extra
            if gap == blocks - 1:
                far[big_i * b + b - 1, big_j, 3] = -extra
    return dense, local, moments, far


THIRD = NX // 3
ROOT = np.sqrt(3.0)


def thirds_forward(m):
    rows = [m[:THIRD, 0::3]]
    for r in (1, 2):
        top = m[:THIRD, r::3]
        rows += [top, (2.0 * m[THIRD:2 * THIRD, r::3] + top) / ROOT]
    return np.concatenate(rows, 0)


def thirds_backward(m):
    top = np.concatenate([m[1::3, :THIRD], m[2::3, :THIRD]], 0)
    next_third = np.concatenate([m[1::3, THIRD:2 * THIRD], m[2::3, THIRD:2 * THIRD]], 0)
    return np.concatenate([m[0::3, :THIRD], top, (2.0 * next_third + top) / ROOT], 0)


def halves(a):
    a = np.asarray(a, np.float32)
    hi = a.astype(jnp.bfloat16)
    lo = (a - hi.astype(np.float32)).astype(jnp.bfloat16)
    return hi, lo


RATIO = (np.sqrt(5.0) - 3.0) / 2.0
TAIL, EDGE = 25.0 / 12.0, -1.0 / 12.0


def mode_tables():
    wx, wz = wave(NX)[np.arange(NX).reshape(256, 3).T.reshape(-1)], wave(NZ)
    kappa = np.sqrt(wz[:, None] ** 2 + wx[None, :] ** 2).reshape(-1)
    null = kappa == 0.0
    kap = np.where(null, 1.0, kappa)
    c = np.stack([np.full_like(kap, 1 / 36), kap / 3 + 7 / 9, kap, kap / 3 - 7 / 9, np.full_like(kap, -1 / 36)], 1)
    companion = np.zeros((kap.size, 4, 4))
    companion[:, 0, :] = -c[:, 1:] / c[:, :1]
    companion[:, 1, 0] = companion[:, 2, 1] = companion[:, 3, 2] = 1.0
    z = np.sort(np.linalg.eigvals(companion).real, 1)
    c = c[:, :, None]
    for _ in range(3):
        value = (((c[:, 0] * z + c[:, 1]) * z + c[:, 2]) * z + c[:, 3]) * z + c[:, 4]
        slope = ((4 * c[:, 0] * z + 3 * c[:, 1]) * z + 2 * c[:, 2]) * z + c[:, 3]
        z = z - value / slope
    z = np.stack([z[:, 3], 1 / z[:, 1], z[:, 2], 1 / z[:, 0]], 1)
    cos = (z + 1 / z) / 2
    lead = 14 / 9 + cos / 9
    slope = -2 * cos * lead**2 + (1 - cos**2) * 2 * lead / 9 + kap[:, None] ** 2 * 2 * (1 + 2 * cos / 3) * 2 / 3
    a = -((1 + 2 * cos / 3) ** 2) / slope * 2 * z / (1 - z * z)
    a = np.where(null[:, None], 0.0, a) / float(NX * NZ)
    turn = np.where(null[:, None], 1.0, z**BY)
    close = np.where(null[:, None], 1.0, 1 / (1 - z**NY))
    z = np.where(null[:, None], 0.5, z)

    def place(t):
        t = t.reshape(2, ROWS, NX, -1)
        out = np.zeros((COLS, ROWS, 3, 128, t.shape[-1]))
        for c in range(COLS):
            low, high = t[:, :, 128 * c:128 * c + 128], t[:, :, 512 + 64 * c:576 + 64 * c]
            out[c, :, 0], out[c, :, 1] = low[0], low[1]
            out[c, :, 2, :64], out[c, :, 2, 64:] = high[0], high[1]
        return out

    local = place(np.concatenate([z, a], 1)).transpose(0, 4, 2, 1, 3)
    cycle = place(np.concatenate([turn, turn, close, close], 1))
    cycle = cycle.transpose(0, 1, 2, 4, 3).reshape(COLS, ROWS, 3, 2, 8, 128).transpose(0, 1, 3, 2, 4, 5)
    return local.astype(np.float32), np.ascontiguousarray(cycle.reshape(COLS, ROWS, 2, 24, 128)).astype(np.float32)


@functools.lru_cache(maxsize=None)
def null_inverse():
    _, local, moments, _ = split_derivative(NY, BY)
    return np.linalg.pinv(np.concatenate([local, moments], 0))


@functools.lru_cache(maxsize=None)
def constants():
    dense_x = split_derivative(NX, BY)[0]
    _, loc_y, mom_y, far_y = split_derivative(NY, BY)
    _, loc_z, mom_z, far_z = split_derivative(NZ, BZ)
    hx, hy, hz = hartley(NX), hartley(NY), hartley(NZ)
    eye_y, eye_z = np.eye(BY), np.eye(BZ)
    lv_q, lv_m = np.kron(loc_y, eye_z), np.kron(mom_y, eye_z)
    lw_q, lw_m = np.kron(eye_y, loc_z), np.kron(eye_y, mom_z)
    left_v = np.concatenate([lv_m, lv_q, np.zeros_like(lw_m)], 0)
    left_w = np.concatenate([np.zeros_like(lv_m), lw_q, lw_m], 0)
    far_hz = np.einsum("kz,zcm->kcm", hz, far_z)
    wz = np.zeros((6, NZ, 224))
    for y in range(6):
        wz[y, :, :NZ] = hz
        wide = np.zeros((NZ, COLS, 6, 4))
        wide[:, :, y, :] = far_hz
        wz[y, :, NZ:] = wide.reshape(NZ, 96)
    out = {}
    for name, value in (
        ("hx", thirds_forward(hx)),
        ("fwd_dx", thirds_forward(dense_x.T @ hx)),
        ("hx_back", thirds_backward(hx)),
        ("bwd_dx", thirds_backward(hx @ dense_x.T)),
        ("left", np.concatenate([left_v, left_w], 1)),
        ("left_tv", left_v[:512].T),
        ("left_tw", left_w[128:].T),
        ("wz", wz),
        ("wz_t", np.swapaxes(wz, 1, 2)),
    ):
        out[name] = halves(value)
    out["local"], out["cycle"] = mode_tables()
    return out


def two(a):
    hi = a.astype(BF16)
    return hi, (a - hi.astype(F32)).astype(BF16)


def dot(a, b):
    return jnp.dot(a, b, preferred_element_type=F32)


def dot3(a, b):
    return dot(a[0], b[0]) + (dot(a[0], b[1]) + dot(a[1], b[0]))


def low_half(shape):
    return lax.broadcasted_iota(jnp.int32, shape, len(shape) - 1) < 64


def join(first, second):
    return jnp.where(low_half(first.shape), first, pltpu.roll(second, 64, 1))


def join_high(first, second):
    return jnp.where(low_half(first.shape), pltpu.roll(first, 64, 1), second)


def set_inflow(place, cells, speed, upward):
    def step(t, carry):
        y = t // 2
        row = place[0] * BY + y
        k = (16 * row + 4 * place[1]) // 3 + t % 2
        rel = cells[k] - (row * NZ + place[1] * BZ) * NX
        inside = (rel >= 0) & (rel < BZ * NX)
        rel = jnp.where(inside, rel, 0)
        line = rel // NX
        x = jnp.where(inside, rel - line * NX, -1)
        at = pl.ds(y * BZ + line, 1)
        lanes = lax.broadcasted_iota(jnp.int32, (1, NX), 1)
        upward[at, :] = jnp.where(lanes == x, speed[k], upward[at, :])
        return carry

    lax.fori_loop(0, 2 * BY, step, 0)


def fold(parts):
    a, b, c = parts
    return a + (b + c), a - 0.5 * (b + c), (0.5 * ROOT).item() * (b - c)


def unfold(a, b, q):
    low, high = a - 0.5 * b, (0.5 * ROOT).item() * q
    return a + b, low + high, low - high


def deal(place, blocks, outs):
    for d, out in enumerate(outs):
        out[...] = blocks[place[1] ^ d]


def collect(place, ins, blocks):
    for d, block in enumerate(ins):
        blocks[place[1] ^ d] = block[...]


def exchange(blocks):
    moved = {d: lax.ppermute(blocks[d], "col", [(c, c ^ d) for c in range(COLS)]) for d in (2, 3, 1)}
    return [blocks[0], moved[1], moved[2], moved[3]]


def forward_x(place, cells, speed, u_in, v_in, w_in, solid_in, lh_in, ll_in, hh_in, hl_in, dh_in, dl_in,
              o0, o1, o2, o3, out, u, v, w, solid, lh, ll, hh, hl, dh, dl, sems):
    pairs = [(solid_in, solid), (w_in, w), (lh_in, lh), (ll_in, ll), (v_in, v),
             (hh_in, hh), (hl_in, hl), (u_in, u), (dh_in, dh), (dl_in, dl)]
    copies = [pltpu.make_async_copy(a, b, sems.at[i]) for i, (a, b) in enumerate(pairs)]
    for copy in copies:
        copy.start()
    for copy in copies[:2]:
        copy.wait()
    fluid = (1 - solid[...]).astype(F32)
    w[...] = w[...] * fluid
    set_inflow(place, cells, speed, w)
    for copy in copies[2:5]:
        copy.wait()
    left = (lh[...], ll[...])
    thirds = []
    for n in range(3):
        at = slice(n * 256, (n + 1) * 256)
        both = jnp.concatenate([v[:, at] * fluid[:, at], w[:, at]], 0)
        thirds.append(dot3(left, two(both)))
    c0, c, d = fold(thirds)
    all_0, all_1 = two(c0), two(jnp.concatenate([c, d], 1))
    for copy in copies[5:8]:
        copy.wait()
    c0, c, d = fold([u[:, n * 256:(n + 1) * 256] * fluid[:, n * 256:(n + 1) * 256] for n in range(3)])
    east_0, east_1 = two(c0), two(jnp.concatenate([c, d], 1))
    for copy in copies[8:]:
        copy.wait()
    for n in range(3):
        at = slice(0, 256) if n == 0 else slice(512 * n - 256, 512 * n + 256)
        r = dot3(all_1 if n else all_0, (hh[at, :], hl[at, :]))
        d = dot3(east_1 if n else east_0, (dh[at, :], dl[at, :]))
        for t in range(2):
            own = slice(t * 128, (t + 1) * 128)
            a = jnp.concatenate([r[128:320, own] + d[:192, own], r[0:64, own], r[512:536, own]], 0)
            b = jnp.concatenate([r[320:512, own] + d[192:, own], r[64:128, own], r[536:560, own]], 0)
            c = 2 * n + t
            if c < 4:
                out[c, :, 0:128] = a
                out[c, :, 128:256] = b
            else:
                c = 2 * (c - 4)
                out[c, :, 256:384] = join(a, b)
                out[c + 1, :, 256:384] = join_high(a, b)
    deal(place, out, (o0, o1, o2, o3))


def backward_x(place, cells, speed, u, v, w, solid, x0, x1, x2, x3, vh, vl, wh, wl, hh, hl, dh, dl,
               uo, vo, wo, x, upward, th, tl, us, vs, ws, sems):
    fluid = (1 - solid[...]).astype(F32)
    upward[...] = w[...] * fluid
    set_inflow(place, cells, speed, upward)
    collect(place, (x0, x1, x2, x3), x)
    for t in range(6):
        if t < 4:
            a, b = x[t, :, 0:128], x[t, :, 128:256]
        else:
            c = 2 * (t - 4)
            e, o = x[c, :, 256:384], x[c + 1, :, 256:384]
            a, b = join(e, o), join_high(e, o)
        rows = [a[192:256], b[192:256], a[0:192], b[0:192], a[256:280], b[256:280]]
        hi, lo = two(jnp.concatenate(rows, 0))
        th[:, t * 128:(t + 1) * 128] = hi
        tl[:, t * 128:(t + 1) * 128] = lo

    def back(rows, mh, ml):
        first, rest = (th[rows, 0:256], tl[rows, 0:256]), (th[rows, 256:768], tl[rows, 256:768])
        return unfold(*[
            dot3(left, (mh[at, :], ml[at, :]))
            for left, at in ((first, slice(0, 256)), (rest, slice(256, 768)), (rest, slice(768, 1280)))
        ])

    p = back(slice(0, 560), hh, hl)
    d = back(slice(128, 512), dh, dl)
    copies = []

    def send(i, n, stage, target):
        at = pl.ds(n * 256, 256)
        copies.append(pltpu.make_async_copy(stage.at[:, at], target.at[:, at], sems.at[3 * i + n]))
        copies[-1].start()

    for n in range(3):
        at = slice(n * 256, (n + 1) * 256)
        us[:, at] = u[:, at] * fluid[:, at] - d[n]
        send(0, n, us, uo)
    for n in range(3):
        at = slice(n * 256, (n + 1) * 256)
        hi, lo = two(p[n])
        vs[:, at] = v[:, at] * fluid[:, at] + dot3((vh[...], vl[...]), (hi[0:512], lo[0:512]))
        send(1, n, vs, vo)
        ws[:, at] = upward[:, at] + dot3((wh[...], wl[...]), (hi[128:560], lo[128:560]))
        send(2, n, ws, wo)
    for copy in copies:
        copy.wait()


def forward_z(place, x0, x1, x2, x3, wh, wl, table, out, keep, x, sem):
    copy = pltpu.make_async_copy(table.at[place[1]], keep.at[pl.ds(16, 8)], sem)
    copy.start()
    collect(place, (x0, x1, x2, x3), x)
    marks = [x[c, 256:280, :] for c in range(COLS)]
    for y in range(8):
        own = [x[c, y * 32:(y + 1) * 32, :] for c in range(COLS)]
        if y < 6:
            z = dot3((wh[y], wl[y]), two(jnp.concatenate(own + marks, 0)))
            planes = (y, 6 + y)
        else:
            z = dot3((wh[0, :, 0:128], wl[0, :, 0:128]), two(jnp.concatenate(own, 0)))
            planes = (6 + y, 8 + y)
        a, b = z[0:64], z[64:128]
        for half, plane in enumerate(planes):
            tile = slice(half * 128, (half + 1) * 128)
            pick = join_high if half else join
            keep[plane, 0] = a[:, tile]
            keep[plane, 1] = b[:, tile]
            keep[plane, 2] = pick(a[:, 256:384], b[:, 256:384])
    copy.wait()

    def step(j, carry):
        for t in range(3):
            at = lambda p: keep[p, t, pl.ds(8 * j, 8), :]
            q = [at(p) for p in range(BY)]
            plus, minus, last, first = [at(BY + p) for p in range(4)]
            for k in range(4):
                z = at(16 + k)
                near, far = tails(z)
                right = -z * (near * minus + EDGE * first)
                left = z * (near * plus + EDGE * last)
                for i in range(BY):
                    right = z * (right + q[i])
                    left = z * (left + q[BY - 1 - i])
                right = right + (z * far * plus + EDGE * last)
                left = left - (z * far * minus + EDGE * first)
                out[pl.ds(192 * j + 8 * t + k, 8, stride=24), :] = right
                out[pl.ds(192 * j + 8 * t + 4 + k, 8, stride=24), :] = left
        return carry

    lax.fori_loop(0, ROWS // 8, step, 0)
    for t in range(2):
        null = keep[20, t, 0:8, :] == 0.0
        sums = null_sums([keep[p, t, 0:8, :] for p in range(16)])
        for k in range(2):
            for m in (k, 4 + k):
                at = pl.ds(8 * t + m, 8, stride=24)
                out[at, :] = jnp.where(null, sums[k], out[at, :])


def weigh(weights, values):
    return sum(float(w) * value for w, value in zip(weights, values))


def null_sums(planes):
    inverse = null_inverse()
    return weigh(inverse.sum(0), planes), weigh(((-1.0) ** np.arange(BY)) @ inverse, planes)


def null_planes(planes, totals):
    inverse = null_inverse()
    v = [weigh(inverse[i], planes) - (totals[0] + (-1.0) ** i * totals[1]) / float(NY) for i in range(BY)]
    return [weigh(-inverse[:, p] / float(NX * NZ), v) for p in range(16)]


def tails(z):
    return TAIL * RATIO / (1.0 - RATIO * z), TAIL * RATIO / (z - RATIO)


def couple_blocks(place, m, cycle, out, own, hold, sem):
    copy = pltpu.make_async_copy(cycle.at[place[1], place[0]], own, sem)
    copy.start()
    copy.wait()
    ratio = [own[0, 8 * t:8 * t + 8, :] for t in range(3)]
    close = [own[1, 8 * t:8 * t + 8, :] for t in range(3)]
    upper = lax.broadcasted_iota(jnp.int32, (8, 128), 0) < 4

    def advance(j, s):
        new = []
        for t in range(3):
            rows = slice(8 * t, 8 * t + 8)
            new.append(ratio[t] * s[t] + jnp.where(upper, m[j, rows, :], m[ROWS - 1 - j, rows, :]))
        return tuple(new)

    zero = jnp.zeros((8, 128), F32)
    s = lax.fori_loop(0, ROWS, advance, (zero,) * 3, unroll=8)
    s = tuple(s[t] * close[t] for t in range(3))

    def store(j, s):
        for t in range(3):
            hold[j, 8 * t:8 * t + 8, :] = s[t]
        return advance(j, s)

    lax.fori_loop(0, ROWS, store, s, unroll=8)

    def merge(j, carry):
        for t in range(3):
            rows = slice(8 * t, 8 * t + 8)
            out[j, rows, :] = jnp.where(upper, hold[j, rows, :], hold[ROWS - 1 - j, rows, :])
        return carry

    lax.fori_loop(0, ROWS, merge, 0, unroll=8)


def backward_z(place, s, keep, wh, wl, o0, o1, o2, o3, out, made):
    def step(j, carry):
        for t in range(3):
            at = lambda p: keep[p, t, pl.ds(8 * j, 8), :]
            state = lambda m: s[pl.ds(192 * j + 8 * t + m, 8, stride=24), :]
            q = [at(p) for p in range(BY)]
            plus, minus, last, first = [at(BY + p) for p in range(4)]
            p = [0.0] * BY
            g = [0.0] * 4
            for k in range(4):
                z, a = at(16 + k), at(20 + k)
                near, far = tails(z)
                from_left, from_right = state(k), state(4 + k)
                right = from_left - z * (near * minus + EDGE * first)
                left = from_right + z * (near * plus + EDGE * last)
                for i in range(BY):
                    right = (right if i == 0 else z * right) + q[i]
                    p[i] = p[i] - a * right
                    back = BY - 1 - i
                    p[back] = p[back] - a * left
                    left = z * (left + q[back])
                right = z * right + (z * far * plus + EDGE * last)
                left = left - (z * far * minus + EDGE * first)
                inverse = 1.0 / z
                g[0] = g[0] - a * (near * right + far * from_right)
                g[1] = g[1] + a * (near * left + far * from_left)
                g[2] = g[2] - a * EDGE * (right + inverse * from_right)
                g[3] = g[3] + a * EDGE * (left + inverse * from_left)
            for i, value in enumerate(p + g):
                made[i, t, pl.ds(8 * j, 8), :] = value
        return carry

    lax.fori_loop(0, ROWS // 8, step, 0)
    for t in range(2):
        null = keep[20, t, 0:8, :] == 0.0
        planes = [keep[p, t, 0:8, :] for p in range(16)]
        own = null_sums(planes)
        state = lambda m: s[pl.ds(8 * t + m, 8, stride=24), :]
        totals = [(own[k] + state(k) + state(4 + k)) / 3.0 for k in range(2)]
        for i, value in enumerate(null_planes(planes, totals)):
            made[i, t, 0:8, :] = jnp.where(null, value, made[i, t, 0:8, :])
    total = None
    for y in range(8):
        planes = (y, 6 + y) if y < 6 else (6 + y, 8 + y)
        t = [[made[p, k] for k in range(3)] for p in planes]
        low = jnp.concatenate([t[0][0], t[1][0], join(t[0][2], t[1][2])], 1)
        high = jnp.concatenate([t[0][1], t[1][1], join_high(t[0][2], t[1][2])], 1)
        z = two(jnp.concatenate([low, high], 0))
        if y < 6:
            r = dot3((wh[y], wl[y]), z)
            total = r[128:224] if total is None else total + r[128:224]
        else:
            r = dot3((wh[0, 0:128, :], wl[0, 0:128, :]), z)
        for c in range(COLS):
            out[c, y * 32:(y + 1) * 32, :] = r[c * 32:(c + 1) * 32]
    for c in range(COLS):
        out[c, 256:280, :] = total[c * 24:(c + 1) * 24]
    deal(place, out, (o0, o1, o2, o3))


def call(kernel, out_shape, args, scratch=(), scalars=0, anywhere=(), out_space=pltpu.VMEM, vmem=48):
    spec_v = pl.BlockSpec(memory_space=pltpu.VMEM)
    spec_s = pl.BlockSpec(memory_space=pltpu.SMEM)
    many = isinstance(out_shape, (tuple, list))
    return pl.pallas_call(
        kernel,
        out_shape=out_shape,
        in_specs=[
            spec_s if i < scalars else pl.BlockSpec(memory_space=pltpu.HBM) if i in anywhere else spec_v
            for i in range(len(args))
        ],
        out_specs=[pl.BlockSpec(memory_space=out_space)] * len(out_shape) if many else spec_v,
        scratch_shapes=list(scratch),
        compiler_params=pltpu.CompilerParams(vmem_limit_bytes=vmem * 2**20),
        name=kernel.__name__,
    )(*args)


def body(east_flow, north_flow, upward_flow, solid, inflow_cells, inflow_speed):
    k = constants()
    row, col = lax.axis_index("row"), lax.axis_index("col")
    place = jnp.stack([row, col]).astype(jnp.int32)
    flat = (BY * BZ, NX)
    fields = [a.reshape(flat) for a in (east_flow, north_flow, upward_flow, solid)]
    sds = jax.ShapeDtypeStruct
    mov = (COLS, 280, 384)
    x = call(
        forward_x, [sds(mov[1:], F32)] * COLS,
        [place, inflow_cells, inflow_speed, *fields, *k["left"], *k["hx"], *k["fwd_dx"]],
        [pltpu.VMEM(mov, F32)] + [pltpu.VMEM(flat, F32)] * 3 + [pltpu.VMEM(flat, jnp.int32)] + [pltpu.VMEM((560, NX), BF16)] * 2
        + [pltpu.VMEM((1280, 256), BF16)] * 4 + [pltpu.SemaphoreType.DMA((10,))], 3, range(3, 13), vmem=60,
    )
    x = exchange(x)
    m, keep = call(
        forward_z, (sds((ROWS * 24, 128), F32), sds((24, 3, ROWS, 128), F32)),
        [place, *x, *k["wz"], k["local"]], [pltpu.VMEM(mov, F32), pltpu.SemaphoreType.DMA], 1, anywhere=(7,),
    )
    m = lax.all_to_all(m.reshape(ROWS, 24, 128), "row", 0, 0, tiled=True)
    m = call(
        couple_blocks, sds((ROWS, 24, 128), F32), [place, m, k["cycle"]],
        [pltpu.VMEM((2, 24, 128), F32), pltpu.VMEM((ROWS, 24, 128), F32), pltpu.SemaphoreType.DMA],
        1, anywhere=(2,), vmem=16,
    )
    m = lax.all_to_all(m, "row", 0, 0, tiled=True).reshape(ROWS * 24, 128)
    x = call(
        backward_z, [sds(mov[1:], F32)] * COLS, [place, m, keep, *k["wz_t"]],
        [pltpu.VMEM(mov, F32), pltpu.VMEM((16, 3, ROWS, 128), F32)], 1,
    )
    x = exchange(x)
    outs = call(
        backward_x, [sds(flat, F32)] * 3,
        [place, inflow_cells, inflow_speed, *fields, *x, *k["left_tv"], *k["left_tw"], *k["hx_back"], *k["bwd_dx"]],
        [pltpu.VMEM(mov, F32), pltpu.VMEM(flat, F32), pltpu.VMEM((560, NX), BF16), pltpu.VMEM((560, NX), BF16)]
        + [pltpu.VMEM(flat, F32)] * 3 + [pltpu.SemaphoreType.DMA((9,))], 3, out_space=pltpu.HBM,
    )
    return tuple(o.reshape(BY, BZ, NX) for o in outs)


def solution(mesh):
    spec = P("row", "col", None)
    return jax.shard_map(
        body, mesh=mesh, in_specs=(spec,) * 4 + (P(), P()), out_specs=(spec,) * 3, check_vma=False
    )
```

```python
import functools

import jax
import jax.numpy as jnp
import numpy as np
from jax import lax
from jax.experimental import pallas as pl
from jax.experimental.pallas import tpu as pltpu
from jax.sharding import PartitionSpec as P

NX, NY, NZ = 768, 768, 128
ROWS, COLS = 64, 4
BY, BZ = NY // ROWS, NZ // COLS
F32, BF16 = jnp.float32, jnp.bfloat16


def wave(n):
    t = 2.0 * np.pi * np.arange(n) / n
    w = (14.0 / 9.0 * np.sin(t) + np.sin(2.0 * t) / 18.0) / (1.0 + 2.0 / 3.0 * np.cos(t))
    w[0] = 0.0
    w[n // 2] = 0.0
    return w


def hartley(n):
    k = np.arange(n)
    a = 2.0 * np.pi / n * (np.outer(k, k) % n)
    return np.cos(a) + np.sin(a)


def split_derivative(n, b):
    k = np.arange(n)
    first = -(np.sin(2.0 * np.pi / n * (np.outer(k, k) % n)) @ wave(n)) / n
    d = -first
    d = -d
    r = (np.sqrt(5.0) - 3.0) / 2.0
    dense = d[(k[:, None] - k[None, :]) % n]
    blocks = n // b
    local = dense[:b, :b]
    c0 = d[2] * (1.0 - r**n) / (r**2 - r ** (n - 2))
    c0 = c0 / (1.0 - r**n)
    extra = d[1] - c0 * (r - r ** (n - 1))
    j = np.arange(b)
    moments = np.zeros((4, b))
    moments[0] = r ** (b - 1 - j)
    moments[1] = r**j
    moments[2, b - 1] = 1.0
    moments[3, 0] = 1.0
    far = np.zeros((n, blocks, 4))
    i = np.arange(b)
    for big_i in range(blocks):
        for big_j in range(blocks):
            if big_i == big_j:
                continue
            gap = (big_i - big_j) % blocks
            rows = slice(big_i * b, (big_i + 1) * b)
            far[rows, big_j, 0] = c0 * r ** (b * gap + i - (b - 1)).astype(np.float64)
            far[rows, big_j, 1] = -c0 * r ** (n - b * gap - i).astype(np.float64)
            if gap == 1:
                far[big_i * b, big_j, 2] = extra
            if gap == blocks - 1:
                far[big_i * b + b - 1, big_j, 3] = -extra
    return dense, local, moments, far


THIRD = NX // 3
ROOT = np.sqrt(3.0)


def thirds_forward(m):
    rows = [m[:THIRD, 0::3]]
    for r in (1, 2):
        top = m[:THIRD, r::3]
        rows += [top, (2.0 * m[THIRD:2 * THIRD, r::3] + top) / ROOT]
    return np.concatenate(rows, 0)


def thirds_backward(m):
    top = np.concatenate([m[1::3, :THIRD], m[2::3, :THIRD]], 0)
    next_third = np.concatenate([m[1::3, THIRD:2 * THIRD], m[2::3, THIRD:2 * THIRD]], 0)
    return np.concatenate([m[0::3, :THIRD], top, (2.0 * next_third + top) / ROOT], 0)


def halves(a):
    a = np.asarray(a, np.float32)
    hi = a.astype(jnp.bfloat16)
    lo = (a - hi.astype(np.float32)).astype(jnp.bfloat16)
    return hi, lo


RATIO = (np.sqrt(5.0) - 3.0) / 2.0
TAIL, EDGE = 25.0 / 12.0, -1.0 / 12.0


def mode_tables():
    wx, wz = wave(NX)[np.arange(NX).reshape(256, 3).T.reshape(-1)], wave(NZ)
    kappa = np.sqrt(wz[:, None] ** 2 + wx[None, :] ** 2).reshape(-1)
    null = kappa == 0.0
    kap = np.where(null, 1.0, kappa)
    c = np.stack([np.full_like(kap, 1 / 36), kap / 3 + 7 / 9, kap, kap / 3 - 7 / 9, np.full_like(kap, -1 / 36)], 1)
    companion = np.zeros((kap.size, 4, 4))
    companion[:, 0, :] = -c[:, 1:] / c[:, :1]
    companion[:, 1, 0] = companion[:, 2, 1] = companion[:, 3, 2] = 1.0
    z = np.sort(np.linalg.eigvals(companion).real, 1)
    c = c[:, :, None]
    for _ in range(3):
        value = (((c[:, 0] * z + c[:, 1]) * z + c[:, 2]) * z + c[:, 3]) * z + c[:, 4]
        slope = ((4 * c[:, 0] * z + 3 * c[:, 1]) * z + 2 * c[:, 2]) * z + c[:, 3]
        z = z - value / slope
    z = np.stack([z[:, 3], 1 / z[:, 1], z[:, 2], 1 / z[:, 0]], 1)
    cos = (z + 1 / z) / 2
    lead = 14 / 9 + cos / 9
    slope = -2 * cos * lead**2 + (1 - cos**2) * 2 * lead / 9 + kap[:, None] ** 2 * 2 * (1 + 2 * cos / 3) * 2 / 3
    a = -((1 + 2 * cos / 3) ** 2) / slope * 2 * z / (1 - z * z)
    a = np.where(null[:, None], 0.0, a) / float(NX * NZ)
    turn = np.where(null[:, None], 1.0, z**BY)
    close = np.where(null[:, None], 1.0, 1 / (1 - z**NY))
    z = np.where(null[:, None], 0.5, z)

    def place(t):
        t = t.reshape(2, ROWS, NX, -1)
        out = np.zeros((COLS, ROWS, 3, 128, t.shape[-1]))
        for c in range(COLS):
            low, high = t[:, :, 128 * c:128 * c + 128], t[:, :, 512 + 64 * c:576 + 64 * c]
            out[c, :, 0], out[c, :, 1] = low[0], low[1]
            out[c, :, 2, :64], out[c, :, 2, 64:] = high[0], high[1]
        return out

    local = place(np.concatenate([z, a], 1)).transpose(0, 4, 2, 1, 3)
    cycle = place(np.concatenate([turn, turn, close, close], 1))
    cycle = cycle.transpose(0, 1, 2, 4, 3).reshape(COLS, ROWS, 3, 2, 8, 128).transpose(0, 1, 3, 2, 4, 5)
    return local.astype(np.float32), np.ascontiguousarray(cycle.reshape(COLS, ROWS, 2, 24, 128)).astype(np.float32)


@functools.lru_cache(maxsize=None)
def null_inverse():
    _, local, moments, _ = split_derivative(NY, BY)
    return np.linalg.pinv(np.concatenate([local, moments], 0))


@functools.lru_cache(maxsize=None)
def constants():
    dense_x = split_derivative(NX, BY)[0]
    _, loc_y, mom_y, far_y = split_derivative(NY, BY)
    _, loc_z, mom_z, far_z = split_derivative(NZ, BZ)
    hx, hy, hz = hartley(NX), hartley(NY), hartley(NZ)
    eye_y, eye_z = np.eye(BY), np.eye(BZ)
    lv_q, lv_m = np.kron(loc_y, eye_z), np.kron(mom_y, eye_z)
    lw_q, lw_m = np.kron(eye_y, loc_z), np.kron(eye_y, mom_z)
    left_v = np.concatenate([lv_m, lv_q, np.zeros_like(lw_m)], 0)
    left_w = np.concatenate([np.zeros_like(lv_m), lw_q, lw_m], 0)
    far_hz = np.einsum("kz,zcm->kcm", hz, far_z)
    wz = np.zeros((6, NZ, 224))
    for y in range(6):
        wz[y, :, :NZ] = hz
        wide = np.zeros((NZ, COLS, 6, 4))
        wide[:, :, y, :] = far_hz
        wz[y, :, NZ:] = wide.reshape(NZ, 96)
    out = {}
    for name, value in (
        ("hx", thirds_forward(hx)),
        ("fwd_dx", thirds_forward(dense_x.T @ hx)),
        ("hx_back", thirds_backward(hx)),
        ("bwd_dx", thirds_backward(hx @ dense_x.T)),
        ("left", np.concatenate([left_v, left_w], 1)),
        ("left_tv", left_v[:512].T),
        ("left_tw", left_w[128:].T),
        ("wz", wz),
        ("wz_t", np.swapaxes(wz, 1, 2)),
    ):
        out[name] = halves(value)
    out["local"], out["cycle"] = mode_tables()
    return out


def two(a):
    hi = a.astype(BF16)
    return hi, (a - hi.astype(F32)).astype(BF16)


def dot(a, b):
    return jnp.dot(a, b, preferred_element_type=F32)


def dot3(a, b):
    return dot(a[0], b[0]) + (dot(a[0], b[1]) + dot(a[1], b[0]))


def low_half(shape):
    return lax.broadcasted_iota(jnp.int32, shape, len(shape) - 1) < 64


def join(first, second):
    return jnp.where(low_half(first.shape), first, pltpu.roll(second, 64, 1))


def join_high(first, second):
    return jnp.where(low_half(first.shape), pltpu.roll(first, 64, 1), second)


def set_inflow(place, cells, speed, upward):
    def step(t, carry):
        y = t // 2
        row = place[0] * BY + y
        k = (16 * row + 4 * place[1]) // 3 + t % 2
        rel = cells[k] - (row * NZ + place[1] * BZ) * NX
        inside = (rel >= 0) & (rel < BZ * NX)
        rel = jnp.where(inside, rel, 0)
        line = rel // NX
        x = jnp.where(inside, rel - line * NX, -1)
        at = pl.ds(y * BZ + line, 1)
        lanes = lax.broadcasted_iota(jnp.int32, (1, NX), 1)
        upward[at, :] = jnp.where(lanes == x, speed[k], upward[at, :])
        return carry

    lax.fori_loop(0, 2 * BY, step, 0)


def fold(parts):
    a, b, c = parts
    return a + (b + c), a - 0.5 * (b + c), (0.5 * ROOT).item() * (b - c)


def unfold(a, b, q):
    low, high = a - 0.5 * b, (0.5 * ROOT).item() * q
    return a + b, low + high, low - high


def deal(place, blocks, outs):
    for d, out in enumerate(outs):
        out[...] = blocks[place[1] ^ d]


def collect(place, ins, blocks):
    for d, block in enumerate(ins):
        blocks[place[1] ^ d] = block[...]


def exchange(blocks):
    moved = {d: lax.ppermute(blocks[d], "col", [(c, c ^ d) for c in range(COLS)]) for d in (2, 3, 1)}
    return [blocks[0], moved[1], moved[2], moved[3]]


def forward_x(place, cells, speed, u_in, v_in, w_in, solid_in, lh_in, ll_in, hh_in, hl_in, dh_in, dl_in,
              o0, o1, o2, o3, out, u, v, w, solid, lh, ll, hh, hl, dh, dl, sems):
    pairs = [(solid_in, solid), (w_in, w), (lh_in, lh), (ll_in, ll), (v_in, v),
             (hh_in, hh), (hl_in, hl), (u_in, u), (dh_in, dh), (dl_in, dl)]
    copies = [pltpu.make_async_copy(a, b, sems.at[i]) for i, (a, b) in enumerate(pairs)]
    for copy in copies:
        copy.start()
    for copy in copies[:2]:
        copy.wait()
    fluid = (1 - solid[...]).astype(F32)
    w[...] = w[...] * fluid
    set_inflow(place, cells, speed, w)
    for copy in copies[2:5]:
        copy.wait()
    left = (lh[...], ll[...])
    thirds = []
    for n in range(3):
        at = slice(n * 256, (n + 1) * 256)
        both = jnp.concatenate([v[:, at] * fluid[:, at], w[:, at]], 0)
        thirds.append(dot3(left, two(both)))
    c0, c, d = fold(thirds)
    all_0, all_1 = two(c0), two(jnp.concatenate([c, d], 1))
    for copy in copies[5:8]:
        copy.wait()
    c0, c, d = fold([u[:, n * 256:(n + 1) * 256] * fluid[:, n * 256:(n + 1) * 256] for n in range(3)])
    east_0, east_1 = two(c0), two(jnp.concatenate([c, d], 1))
    for copy in copies[8:]:
        copy.wait()
    for n in range(3):
        at = slice(0, 256) if n == 0 else slice(512 * n - 256, 512 * n + 256)
        r = dot3(all_1 if n else all_0, (hh[at, :], hl[at, :]))
        d = dot3(east_1 if n else east_0, (dh[at, :], dl[at, :]))
        for t in range(2):
            own = slice(t * 128, (t + 1) * 128)
            a = jnp.concatenate([r[128:320, own] + d[:192, own], r[0:64, own], r[512:536, own]], 0)
            b = jnp.concatenate([r[320:512, own] + d[192:, own], r[64:128, own], r[536:560, own]], 0)
            c = 2 * n + t
            if c < 4:
                out[c, :, 0:128] = a
                out[c, :, 128:256] = b
            else:
                c = 2 * (c - 4)
                out[c, :, 256:384] = join(a, b)
                out[c + 1, :, 256:384] = join_high(a, b)
    copies = [
        pltpu.make_async_copy(out.at[place[1] ^ d], target, sems.at[10 + d])
        for d, target in enumerate((o0, o1, o2, o3))
    ]
    for copy in copies:
        copy.start()
    for copy in copies:
        copy.wait()


def backward_x(place, cells, speed, u, v, w, solid, x0, x1, x2, x3, vh, vl, wh, wl, hh, hl, dh, dl,
               uo, vo, wo, x, upward, th, tl, us, vs, ws, sems):
    fluid = (1 - solid[...]).astype(F32)
    upward[...] = w[...] * fluid
    set_inflow(place, cells, speed, upward)
    collect(place, (x0, x1, x2, x3), x)
    for t in range(6):
        if t < 4:
            a, b = x[t, :, 0:128], x[t, :, 128:256]
        else:
            c = 2 * (t - 4)
            e, o = x[c, :, 256:384], x[c + 1, :, 256:384]
            a, b = join(e, o), join_high(e, o)
        rows = [a[192:256], b[192:256], a[0:192], b[0:192], a[256:280], b[256:280]]
        hi, lo = two(jnp.concatenate(rows, 0))
        th[:, t * 128:(t + 1) * 128] = hi
        tl[:, t * 128:(t + 1) * 128] = lo

    def back(rows, mh, ml):
        first, rest = (th[rows, 0:256], tl[rows, 0:256]), (th[rows, 256:768], tl[rows, 256:768])
        return unfold(*[
            dot3(left, (mh[at, :], ml[at, :]))
            for left, at in ((first, slice(0, 256)), (rest, slice(256, 768)), (rest, slice(768, 1280)))
        ])

    p = back(slice(0, 560), hh, hl)
    d = back(slice(128, 512), dh, dl)
    copies = []

    def send(i, n, stage, target):
        at = pl.ds(n * 256, 256)
        copies.append(pltpu.make_async_copy(stage.at[:, at], target.at[:, at], sems.at[3 * i + n]))
        copies[-1].start()

    for n in range(3):
        at = slice(n * 256, (n + 1) * 256)
        us[:, at] = u[:, at] * fluid[:, at] - d[n]
        send(0, n, us, uo)
    for n in range(3):
        at = slice(n * 256, (n + 1) * 256)
        hi, lo = two(p[n])
        vs[:, at] = v[:, at] * fluid[:, at] + dot3((vh[...], vl[...]), (hi[0:512], lo[0:512]))
        send(1, n, vs, vo)
        ws[:, at] = upward[:, at] + dot3((wh[...], wl[...]), (hi[128:560], lo[128:560]))
        send(2, n, ws, wo)
    for copy in copies:
        copy.wait()


def forward_z(place, x0, x1, x2, x3, wh, wl, table, out, keep, x, sem):
    copy = pltpu.make_async_copy(table.at[place[1]], keep.at[pl.ds(16, 8)], sem)
    copy.start()
    collect(place, (x0, x1, x2, x3), x)
    marks = [x[c, 256:280, :] for c in range(COLS)]
    for y in range(8):
        own = [x[c, y * 32:(y + 1) * 32, :] for c in range(COLS)]
        if y < 6:
            z = dot3((wh[y], wl[y]), two(jnp.concatenate(own + marks, 0)))
            planes = (y, 6 + y)
        else:
            z = dot3((wh[0, :, 0:128], wl[0, :, 0:128]), two(jnp.concatenate(own, 0)))
            planes = (6 + y, 8 + y)
        a, b = z[0:64], z[64:128]
        for half, plane in enumerate(planes):
            tile = slice(half * 128, (half + 1) * 128)
            pick = join_high if half else join
            keep[plane, 0] = a[:, tile]
            keep[plane, 1] = b[:, tile]
            keep[plane, 2] = pick(a[:, 256:384], b[:, 256:384])
    copy.wait()

    def step(j, carry):
        for t in range(3):
            at = lambda p: keep[p, t, pl.ds(8 * j, 8), :]
            q = [at(p) for p in range(BY)]
            plus, minus, last, first = [at(BY + p) for p in range(4)]
            for k in range(4):
                z = at(16 + k)
                near, far = tails(z)
                right = -z * (near * minus + EDGE * first)
                left = z * (near * plus + EDGE * last)
                for i in range(BY):
                    right = z * (right + q[i])
                    left = z * (left + q[BY - 1 - i])
                right = right + (z * far * plus + EDGE * last)
                left = left - (z * far * minus + EDGE * first)
                out[pl.ds(192 * j + 8 * t + k, 8, stride=24), :] = right
                out[pl.ds(192 * j + 8 * t + 4 + k, 8, stride=24), :] = left
        return carry

    lax.fori_loop(0, ROWS // 8, step, 0)
    for t in range(2):
        null = keep[20, t, 0:8, :] == 0.0
        sums = null_sums([keep[p, t, 0:8, :] for p in range(16)])
        for k in range(2):
            for m in (k, 4 + k):
                at = pl.ds(8 * t + m, 8, stride=24)
                out[at, :] = jnp.where(null, sums[k], out[at, :])


def weigh(weights, values):
    return sum(float(w) * value for w, value in zip(weights, values))


def null_sums(planes):
    inverse = null_inverse()
    return weigh(inverse.sum(0), planes), weigh(((-1.0) ** np.arange(BY)) @ inverse, planes)


def null_planes(planes, totals):
    inverse = null_inverse()
    v = [weigh(inverse[i], planes) - (totals[0] + (-1.0) ** i * totals[1]) / float(NY) for i in range(BY)]
    return [weigh(-inverse[:, p] / float(NX * NZ), v) for p in range(16)]


def tails(z):
    return TAIL * RATIO / (1.0 - RATIO * z), TAIL * RATIO / (z - RATIO)


def couple_blocks(place, m, cycle, out, own, hold, sem):
    copy = pltpu.make_async_copy(cycle.at[place[1], place[0]], own, sem)
    copy.start()
    copy.wait()
    ratio = [own[0, 8 * t:8 * t + 8, :] for t in range(3)]
    close = [own[1, 8 * t:8 * t + 8, :] for t in range(3)]
    upper = lax.broadcasted_iota(jnp.int32, (8, 128), 0) < 4

    def advance(j, s):
        new = []
        for t in range(3):
            rows = slice(8 * t, 8 * t + 8)
            new.append(ratio[t] * s[t] + jnp.where(upper, m[j, rows, :], m[ROWS - 1 - j, rows, :]))
        return tuple(new)

    zero = jnp.zeros((8, 128), F32)
    s = lax.fori_loop(0, ROWS, advance, (zero,) * 3, unroll=8)
    s = tuple(s[t] * close[t] for t in range(3))

    def store(j, s):
        for t in range(3):
            hold[j, 8 * t:8 * t + 8, :] = s[t]
        return advance(j, s)

    lax.fori_loop(0, ROWS, store, s, unroll=8)

    def merge(j, carry):
        for t in range(3):
            rows = slice(8 * t, 8 * t + 8)
            out[j, rows, :] = jnp.where(upper, hold[j, rows, :], hold[ROWS - 1 - j, rows, :])
        return carry

    lax.fori_loop(0, ROWS, merge, 0, unroll=8)


def backward_z(place, s, keep, wh, wl, o0, o1, o2, o3, out, made):
    def step(j, carry):
        for t in range(3):
            at = lambda p: keep[p, t, pl.ds(8 * j, 8), :]
            state = lambda m: s[pl.ds(192 * j + 8 * t + m, 8, stride=24), :]
            q = [at(p) for p in range(BY)]
            plus, minus, last, first = [at(BY + p) for p in range(4)]
            p = [0.0] * BY
            g = [0.0] * 4
            for k in range(4):
                z, a = at(16 + k), at(20 + k)
                near, far = tails(z)
                from_left, from_right = state(k), state(4 + k)
                right = from_left - z * (near * minus + EDGE * first)
                left = from_right + z * (near * plus + EDGE * last)
                for i in range(BY):
                    right = (right if i == 0 else z * right) + q[i]
                    p[i] = p[i] - a * right
                    back = BY - 1 - i
                    p[back] = p[back] - a * left
                    left = z * (left + q[back])
                right = z * right + (z * far * plus + EDGE * last)
                left = left - (z * far * minus + EDGE * first)
                inverse = 1.0 / z
                g[0] = g[0] - a * (near * right + far * from_right)
                g[1] = g[1] + a * (near * left + far * from_left)
                g[2] = g[2] - a * EDGE * (right + inverse * from_right)
                g[3] = g[3] + a * EDGE * (left + inverse * from_left)
            for i, value in enumerate(p + g):
                made[i, t, pl.ds(8 * j, 8), :] = value
        return carry

    lax.fori_loop(0, ROWS // 8, step, 0)
    for t in range(2):
        null = keep[20, t, 0:8, :] == 0.0
        planes = [keep[p, t, 0:8, :] for p in range(16)]
        own = null_sums(planes)
        state = lambda m: s[pl.ds(8 * t + m, 8, stride=24), :]
        totals = [(own[k] + state(k) + state(4 + k)) / 3.0 for k in range(2)]
        for i, value in enumerate(null_planes(planes, totals)):
            made[i, t, 0:8, :] = jnp.where(null, value, made[i, t, 0:8, :])
    total = None
    for y in range(8):
        planes = (y, 6 + y) if y < 6 else (6 + y, 8 + y)
        t = [[made[p, k] for k in range(3)] for p in planes]
        low = jnp.concatenate([t[0][0], t[1][0], join(t[0][2], t[1][2])], 1)
        high = jnp.concatenate([t[0][1], t[1][1], join_high(t[0][2], t[1][2])], 1)
        z = two(jnp.concatenate([low, high], 0))
        if y < 6:
            r = dot3((wh[y], wl[y]), z)
            total = r[128:224] if total is None else total + r[128:224]
        else:
            r = dot3((wh[0, 0:128, :], wl[0, 0:128, :]), z)
        for c in range(COLS):
            out[c, y * 32:(y + 1) * 32, :] = r[c * 32:(c + 1) * 32]
    for c in range(COLS):
        out[c, 256:280, :] = total[c * 24:(c + 1) * 24]
    deal(place, out, (o0, o1, o2, o3))


def call(kernel, out_shape, args, scratch=(), scalars=0, anywhere=(), out_space=pltpu.VMEM, vmem=48):
    spec_v = pl.BlockSpec(memory_space=pltpu.VMEM)
    spec_s = pl.BlockSpec(memory_space=pltpu.SMEM)
    many = isinstance(out_shape, (tuple, list))
    return pl.pallas_call(
        kernel,
        out_shape=out_shape,
        in_specs=[
            spec_s if i < scalars else pl.BlockSpec(memory_space=pltpu.HBM) if i in anywhere else spec_v
            for i in range(len(args))
        ],
        out_specs=[pl.BlockSpec(memory_space=out_space)] * len(out_shape) if many else spec_v,
        scratch_shapes=list(scratch),
        compiler_params=pltpu.CompilerParams(vmem_limit_bytes=vmem * 2**20),
        name=kernel.__name__,
    )(*args)


def body(east_flow, north_flow, upward_flow, solid, inflow_cells, inflow_speed):
    k = constants()
    row, col = lax.axis_index("row"), lax.axis_index("col")
    place = jnp.stack([row, col]).astype(jnp.int32)
    flat = (BY * BZ, NX)
    fields = [a.reshape(flat) for a in (east_flow, north_flow, upward_flow, solid)]
    sds = jax.ShapeDtypeStruct
    mov = (COLS, 280, 384)
    x = call(
        forward_x, [sds(mov[1:], F32)] * COLS,
        [place, inflow_cells, inflow_speed, *fields, *k["left"], *k["hx"], *k["fwd_dx"]],
        [pltpu.VMEM(mov, F32)] + [pltpu.VMEM(flat, F32)] * 3 + [pltpu.VMEM(flat, jnp.int32)] + [pltpu.VMEM((560, NX), BF16)] * 2
        + [pltpu.VMEM((1280, 256), BF16)] * 4 + [pltpu.SemaphoreType.DMA((14,))], 3, range(3, 13), out_space=pltpu.HBM, vmem=60,
    )
    x = exchange(x)
    m, keep = call(
        forward_z, (sds((ROWS * 24, 128), F32), sds((24, 3, ROWS, 128), F32)),
        [place, *x, *k["wz"], k["local"]], [pltpu.VMEM(mov, F32), pltpu.SemaphoreType.DMA], 1, anywhere=(7,),
    )
    m = lax.all_to_all(m.reshape(ROWS, 24, 128), "row", 0, 0, tiled=True)
    m = call(
        couple_blocks, sds((ROWS, 24, 128), F32), [place, m, k["cycle"]],
        [pltpu.VMEM((2, 24, 128), F32), pltpu.VMEM((ROWS, 24, 128), F32), pltpu.SemaphoreType.DMA],
        1, anywhere=(2,), vmem=16,
    )
    m = lax.all_to_all(m, "row", 0, 0, tiled=True).reshape(ROWS * 24, 128)
    x = call(
        backward_z, [sds(mov[1:], F32)] * COLS, [place, m, keep, *k["wz_t"]],
        [pltpu.VMEM(mov, F32), pltpu.VMEM((16, 3, ROWS, 128), F32)], 1,
    )
    x = exchange(x)
    outs = call(
        backward_x, [sds(flat, F32)] * 3,
        [place, inflow_cells, inflow_speed, *fields, *x, *k["left_tv"], *k["left_tw"], *k["hx_back"], *k["bwd_dx"]],
        [pltpu.VMEM(mov, F32), pltpu.VMEM(flat, F32), pltpu.VMEM((560, NX), BF16), pltpu.VMEM((560, NX), BF16)]
        + [pltpu.VMEM(flat, F32)] * 3 + [pltpu.SemaphoreType.DMA((9,))], 3, out_space=pltpu.HBM,
    )
    return tuple(o.reshape(BY, BZ, NX) for o in outs)


def solution(mesh):
    spec = P("row", "col", None)
    return jax.shard_map(
        body, mesh=mesh, in_specs=(spec,) * 4 + (P(), P()), out_specs=(spec,) * 3, check_vma=False
    )
```
